256 devices in a mesh: shot: 32 (over x, z_hi, core), tile: 8 (over z_lo, y).
Axes of the slice: x: 4, y: 4, z: 8 (z_hi: 4, z_lo: 2; z = z_hi * 2 + z_lo), core: 2. Of those that a mesh axis runs over, the one named last changes fastest.
Arguments:
- velocity: float32 [128, 64, 128], P('shot', 'tile'), may hold values from 0.2 to 0.55
- density: float32 [128, 64, 128], P('shot', 'tile'), may hold values from 1 to 3
- anchors: int32 [32], replicated, may hold values from 0 to 16
- src_state: float32 [4, 2048, 64, 128], P(None, 'shot', 'tile'), may hold values from -6 to 6
- rcv_state: float32 [4, 2048, 64, 128], P(None, 'shot', 'tile'), may hold values from -6 to 6
- src_pos: int32 [32, 16], P('shot'), may hold values from 0 to 524287
- wavelet: float32 [32, 16, 4], P('shot'), may hold values from -6 to 6
- rec_pos: int32 [32, 128], P('shot'), may hold values from 0 to 524287
- traces: float32 [32, 128, 4], P('shot'), may hold values from -6 to 6
Outputs:
- stacked_image: float32 [128, 64, 128], P('shot', 'tile')
The draws below stay inside these ranges and needn't reach their ends.
Inputs may be any that keep to these rules, and one draw needn't show every extreme that they name: `anchors`: each aperture covers 16 whole strips of the slab.
All inputs are finite; a program needn't handle non-finite values.
Results may differ from the reference program's by a relative error of at most 0.00002.
Values sent between devices are 32-bit elements; how exact they have to be, the bound alone decides.
No kernel may reach another device: no remote copies, remote signals or barrier semaphores. Data moves between devices by JAX's collectives and lax.ppermute only.
A program may use at most 64 MiB of HBM per device.

```python
import math
import jax
import jax.numpy as jnp
from jax import lax

SX = 4
NZ = 128
K = 16
STEPS = 4
NSRC = 16
NREC = 128
MX = 128
MY = 64
AX = 64
N_SHOT = 32


def with_ends(drawn, key, low, top_value):
    extent = drawn.shape
    index_at = [jax.random.randint(jax.random.fold_in(key, axis), (), 0, extent[axis]) for axis in range(len(extent))]
    drawn = drawn.at[tuple(index_at)].set(low)
    longest = extent.index(max(extent))
    index_at[longest] = (index_at[longest] + 1) % extent[longest]
    return drawn.at[tuple(index_at)].set(top_value)


def levels(key, dims, pieces, smallest, high):
    level = 1.0
    for dim, parts in pieces:
        draws = jax.random.uniform(jax.random.fold_in(jax.random.fold_in(key, 6), dim), (parts,), jnp.float32, smallest / len(pieces), high / len(pieces))
        level = level * jnp.repeat(jnp.exp(draws), dims[dim] // parts).reshape((-1,) + (1,) * (len(dims) - 1 - dim))
    return level


def gaussian(own_key, dims, scale, bound, split=(), dtype=jnp.bfloat16):
    drawn = scale * jax.random.normal(own_key, dims, jnp.float32)
    if split:
        drawn = drawn * levels(own_key, dims, split, -0.22, 0.18)
    return jnp.clip(drawn, -bound, bound).astype(dtype)


def setup_inputs(seed: int = 0) -> dict:
    seeds = jax.random.split(jax.random.key(seed), 10)
    return {
        "velocity": jnp.clip(jnp.exp(math.log(0.55) - 1.011601 * jax.random.uniform(seeds[0], (MX, MY, NZ), jnp.float32) ** levels(seeds[0], (MX, MY, NZ), ((0, 32), (1, 8)), -0.2, 0.2)), 0.2, 0.55),
        "density": jnp.clip(jnp.exp(math.log(3.0) - 1.0986123 * jax.random.uniform(seeds[1], (MX, MY, NZ), jnp.float32) ** levels(seeds[1], (MX, MY, NZ), ((0, 32), (1, 8)), -0.2, 0.2)), 1.0, 3.0),
        "anchors": with_ends(jax.random.randint(seeds[2], (N_SHOT,), 0, N_SHOT - K + 1), jax.random.fold_in(seeds[2], 1), 0, N_SHOT - K).astype(jnp.int32),
        "src_state": gaussian(seeds[3], (4, N_SHOT * AX, MY, NZ), 1.0, 6.0, ((1, 32), (2, 8)), jnp.float32),
        "rcv_state": gaussian(seeds[4], (4, N_SHOT * AX, MY, NZ), 1.0, 6.0, ((1, 32), (2, 8)), jnp.float32),
        "src_pos": with_ends(jax.random.randint(seeds[5], (N_SHOT, NSRC), 0, AX * MY * NZ), jax.random.fold_in(seeds[5], 1), 0, (AX * MY * NZ) - 1).astype(jnp.int32),
        "wavelet": gaussian(seeds[6], (N_SHOT, NSRC, STEPS), 1.0, 6.0, ((0, 32),), jnp.float32),
        "rec_pos": with_ends(jax.random.randint(seeds[7], (N_SHOT, NREC), 0, AX * MY * NZ), jax.random.fold_in(seeds[7], 1), 0, (AX * MY * NZ) - 1).astype(jnp.int32),
        "traces": gaussian(seeds[8], (N_SHOT, NREC, STEPS), 1.0, 6.0, ((0, 32),), jnp.float32),
    }


def next_cell(field, dimension):
    length = field.shape[dimension]
    remainder = lax.slice_in_dim(field, 1, length, axis=dimension)
    border = jnp.zeros_like(lax.slice_in_dim(field, 0, 1, axis=dimension))
    return jnp.concatenate([remainder, border], axis=dimension)


def prev_cell(field, dimension):
    length = field.shape[dimension]
    remainder = lax.slice_in_dim(field, 0, length - 1, axis=dimension)
    border = jnp.zeros_like(lax.slice_in_dim(field, 0, 1, axis=dimension))
    return jnp.concatenate([border, remainder], axis=dimension)


def velocity_step(pressure, vel_x, vel_y, vel_z, buoyancy):
    vel_x = vel_x - buoyancy * (next_cell(pressure, 0) - pressure)
    vel_y = vel_y - buoyancy * (next_cell(pressure, 1) - pressure)
    vel_z = vel_z - buoyancy * (next_cell(pressure, 2) - pressure)
    return vel_x, vel_y, vel_z


def pressure_step(pressure, vel_x, vel_y, vel_z, modulus):
    spread = (vel_x - prev_cell(vel_x, 0)) + (vel_y - prev_cell(vel_y, 1)) + (vel_z - prev_cell(vel_z, 2))
    return pressure - modulus * spread


def inject_points(pressure, position, amplitudes):
    cell_x = position // (MY * NZ)
    cell_y = (position // NZ) % MY
    cell_z = position % NZ
    return pressure.at[cell_x, cell_y, cell_z].add(amplitudes)


def reference(velocity, density, anchors, src_state, rcv_state, src_pos, wavelet, rec_pos, traces):
    def run_group(group_index, slab):
        row_start = anchors[group_index] * SX
        vel = lax.dynamic_slice_in_dim(velocity, row_start, AX, 0)
        den = lax.dynamic_slice_in_dim(density, row_start, AX, 0)
        modulus = den * vel * vel
        buoyancy = 1.0 / den
        forward = lax.dynamic_slice_in_dim(src_state, group_index * AX, AX, 1)
        pressure, vel_x, vel_y, vel_z = forward[0], forward[1], forward[2], forward[3]
        saved_pressure = []
        for step_index in range(STEPS):
            vel_x, vel_y, vel_z = velocity_step(pressure, vel_x, vel_y, vel_z, buoyancy)
            pressure = pressure_step(pressure, vel_x, vel_y, vel_z, modulus)
            pressure = inject_points(pressure, src_pos[group_index], wavelet[group_index][:, step_index])
            saved_pressure.append(pressure)
        backward = lax.dynamic_slice_in_dim(rcv_state, group_index * AX, AX, 1)
        pressure, vel_x, vel_y, vel_z = backward[0], backward[1], backward[2], backward[3]
        correlation = jnp.zeros_like(pressure)
        for step_index in range(STEPS):
            pressure = pressure_step(pressure, vel_x, vel_y, vel_z, modulus)
            vel_x, vel_y, vel_z = velocity_step(pressure, vel_x, vel_y, vel_z, buoyancy)
            pressure = inject_points(pressure, rec_pos[group_index], traces[group_index][:, STEPS - 1 - step_index])
            correlation = correlation + saved_pressure[STEPS - 1 - step_index] * pressure
        correlation = correlation / STEPS
        current = lax.dynamic_slice_in_dim(slab, row_start, AX, 0)
        return lax.dynamic_update_slice_in_dim(slab, current + correlation, row_start, 0)

    blank = jnp.zeros(velocity.shape, jnp.float32)
    return lax.fori_loop(0, N_SHOT, run_group, blank)
```

```python
import functools

import jax
import jax.numpy as jnp
from jax import lax
from jax.experimental import pallas as pl
from jax.experimental.pallas import tpu as pltpu
from jax.sharding import PartitionSpec as P

STEPS = 4
UNROLL = 2
F32 = jnp.float32
ROWS = 64
COLS = 8
DEPTH = 128
PLANES = COLS + 2 * STEPS
NX, NZH, NC, NT = 4, 4, 2, 8

VMEM = pl.BlockSpec(memory_space=pltpu.VMEM)
SMEM = pl.BlockSpec(memory_space=pltpu.SMEM)
ANY = pl.BlockSpec(memory_space=pl.ANY)


def shape(*dims):
    return jax.ShapeDtypeStruct(dims, F32)


def params(mib):
    return pltpu.CompilerParams(vmem_limit_bytes=mib * 1024 * 1024)


def place():
    shot = lax.axis_index("shot")
    return shot // (NZH * NC), (shot // NC) % NZH, shot % NC, shot


def pack_kernel(src, rcv, own, to_prev, to_next):
    lane = lax.broadcasted_iota(jnp.int32, (COLS, DEPTH), 1)
    col = lax.broadcasted_iota(jnp.int32, (COLS, DEPTH), 0)

    def row(x, before):
        after = []
        for f, state in enumerate((src, rcv)):
            p, vx, vy, vz = (state[i, x] for i in range(4))
            spread = vx - before[f]
            spread += vy - jnp.where(col == 0, 0.0, pltpu.roll(vy, 1, 0))
            spread += vz - jnp.where(lane == 0, 0.0, pltpu.roll(vz, 1, 1))
            own[2 * f, pl.ds(x, COLS, stride=ROWS), :] = p
            own[2 * f + 1, pl.ds(x, COLS, stride=ROWS), :] = spread
            last = (COLS - 1)
            to_next[7 + 8 * f - f, pl.ds(x, 1), :] = vy[last:, :]
            after.append(vx)
        return tuple(after)

    zero = jnp.zeros((COLS, DEPTH), F32)
    lax.fori_loop(0, ROWS, row, (zero, zero), unroll=4)

    def plane(f, y):
        return own[f, y * ROWS : (y + 1) * ROWS, :]

    for i, (f, y) in enumerate(
        [(0, 0), (0, 1), (0, 2), (0, 3), (1, 0), (1, 1), (1, 2)]
        + [(2, 0), (2, 1), (2, 2), (3, 0), (3, 1), (3, 2)]
    ):
        to_prev[i] = plane(f, y)
    for i, (f, y) in (
        list(enumerate([(0, 4), (0, 5), (0, 6), (0, 7), (1, 5), (1, 6), (1, 7)]))
        + list(enumerate([(2, 5), (2, 6), (2, 7), (3, 5), (3, 6), (3, 7)], 8))
    ):
        to_next[i] = plane(f, y)


def inject_kernel(src_pos, wavelet, rec_pos, traces, src_out, rec_out):
    src_out[...] = jnp.zeros(src_out.shape, F32)
    rec_out[...] = jnp.zeros(rec_out.shape, F32)
    first = lax.axis_index("tile") * COLS - STEPS
    lane = lax.broadcasted_iota(jnp.int32, (1, DEPTH), 1)
    for pos, amp, out in ((src_pos, wavelet, src_out), (rec_pos, traces, rec_out)):

        def point(k, _, pos=pos, amp=amp, out=out):
            cell = pos[0, k]
            x = cell // (COLS * NT * DEPTH)
            y = (cell // DEPTH) % (COLS * NT) - first
            hit = lane == cell % DEPTH

            @pl.when((y >= 0) & (y < PLANES))
            def _():
                old = [out[s, y, pl.ds(x, 1), :] for s in range(STEPS)]
                for s in range(STEPS):
                    out[s, y, pl.ds(x, 1), :] = old[s] + jnp.where(hit, amp[0, k, s], 0.0)

            return 0

        lax.fori_loop(0, pos.shape[1], point, 0)


def window_kernel(anchors, a0, a1, a2, a3, own, other, strips, sem):
    copies = [pltpu.make_async_copy(a, strips.at[d], sem.at[d]) for d, a in enumerate((a0, a1, a2, a3))]
    for copy in copies:
        copy.start()
    x, z, c, g = place()
    for copy in copies:
        copy.wait()
    for group, out in ((g, own), (g + 1 - 2 * c, other)):
        b = anchors[group]
        first = (b + (c + b) % 2) // 2
        for i in range(8):
            j = first + i
            block = strips.at[(x - j // NZH + NX) % NX, (z - j % NZH + NZH) % NZH]
            vel, den = block[0], block[1]
            out[i, 0] = den * vel * vel
            out[i, 1] = 1.0 / den


def model_kernel(anchors, own, other, out, to_prev, to_next):
    _, _, c, g = place()
    odd = (c + anchors[g]) % 2
    for strips, start in ((own, odd), (other, 1 - odd)):
        for i in range(8):
            for r in range(4):
                x = 4 * (start + 2 * i) + r
                for f in range(2):
                    out[f, pl.ds(x, COLS, stride=ROWS), :] = strips[i, f, r]

    def plane(f, y):
        return out[f, y * ROWS : (y + 1) * ROWS, :]

    for i, (f, y) in enumerate([(0, 0), (0, 1), (0, 2), (1, 0), (1, 1), (1, 2)]):
        to_prev[i] = plane(f, y)
    for i, (f, y) in enumerate([(0, 5), (0, 6), (0, 7), (1, 4), (1, 5), (1, 6), (1, 7)]):
        to_next[i] = plane(f, y)


def march_kernel(
    anchors, own, prev, nxt, mine, model, model_prev, model_next, add_s, add_r,
    keep, send,
    ps, pr, ds, dr, mod, buoy, corr,
):
    vy = (prev.at[7], prev.at[14], mine.at[7], mine.at[14])
    ps[0, 0:4] = prev[0:4]
    ps[0, 4:12] = own[0]
    ps[0, 12:16] = nxt[0:4]
    pr[0, 1:4] = prev[8:11]
    pr[0, 4:12] = own[2]
    pr[0, 12:15] = nxt[7:10]
    for d, f, at, after in ((ds, 0, 4, 4), (dr, 1, 11, 10)):
        d[1:4] = prev[at : at + 3]
        d[4] = own[2 * f + 1, 0] - vy[f][...]
        d[5:12] = own[2 * f + 1, 1:8]
        d[12] = nxt[after] - vy[2 + f][...]
        d[13:15] = nxt[after + 1 : after + 3]
    mod[1:4] = model_prev[0:3]
    mod[4:12] = model[0]
    mod[12:15] = model_next[0:3]
    buoy[0:4] = model_prev[3:7]
    buoy[4:12] = model[1]
    buoy[12:15] = model_next[3:6]
    keep[...] = jnp.zeros(keep.shape, F32)
    send[...] = jnp.zeros(send.shape, F32)

    lane = lax.broadcasted_iota(jnp.int32, (8, DEPTH), 1)
    row = lax.broadcasted_iota(jnp.int32, (8, DEPTH), 0)
    first_lane, last_lane, first_row, last_row = lane == 0, lane == DEPTH - 1, row == 0, row == 7
    blocks = range(ROWS // 8)
    zero = jnp.zeros((8, DEPTH), F32)

    def get(ref, *at):
        return [ref[(*at, slice(8 * v, 8 * v + 8))] for v in blocks]

    def spread_of(p, after, before, b):
        down = [pltpu.roll(p[v], 7, 0) for v in blocks] + [zero]
        flux_y = [b[v] * (after[v] - p[v]) for v in blocks]
        out, last = [], zero
        for v in blocks:
            flux_x = b[v] * (jnp.where(last_row, down[v + 1], down[v]) - p[v])
            flux_z = b[v] * (jnp.where(last_lane, 0.0, pltpu.roll(p[v], DEPTH - 1, 1)) - p[v])
            turned = pltpu.roll(flux_x, 1, 0)
            spread = (flux_x - jnp.where(first_row, last, turned)) + (flux_y[v] - before[v])
            spread += flux_z - jnp.where(first_lane, 0.0, pltpu.roll(flux_z, 1, 1))
            last = turned
            out.append(spread)
        return out, flux_y

    def plane(s, y, carry):
        m, b = get(mod, y), get(buoy, y)
        fields = ((ps, ds, add_s, s), (pr, dr, add_r, STEPS - s)) if s else ((ps, ds, add_s, 0),)
        new, ends = [], []
        for (p_all, d_all, add, amp), (p, before) in zip(fields, carry):
            after = get(p_all, s, y + 1)
            spread, flux = spread_of(p, after, before, b)
            ends.append((after, flux))
            out = []
            for v in blocks:
                cut = slice(8 * v, 8 * v + 8)
                d = d_all[y, cut] - spread[v]
                out.append(p[v] + add[amp, y, cut] - m[v] * d)
                if s < STEPS - 1:
                    d_all[y, cut] = d
                    p_all[s + 1, y, cut] = out[v]
            new.append(out)
        if s == 0:
            for v in blocks:
                cut = slice(8 * v, 8 * v + 8)
                pr[1, y, cut] = pr[0, y, cut] - m[v] * dr[y, cut]
        if s == STEPS - 1:
            for v in blocks:
                cut = slice(8 * v, 8 * v + 8)
                image = new[0][v] * (pr[1, y, cut] + add_r[3, y, cut])
                image += ps[3, y, cut] * (pr[2, y, cut] + add_r[2, y, cut])
                image += ps[2, y, cut] * (pr[3, y, cut] + add_r[1, y, cut])
                image += ps[1, y, cut] * (new[1][v] + add_r[0, y, cut])
                corr[pl.ds(8 * COLS * v + y - STEPS, 8, stride=COLS), :] = image / STEPS
        return ends

    for s in range(STEPS):
        low, high = s + 1, 15 - s
        carry = []
        for p_all in (ps, pr) if s else (ps,):
            here, before, b = get(p_all, s, low), get(p_all, s, low - 1), get(buoy, low - 1)
            carry.append((here, [b[v] * (here[v] - before[v]) for v in blocks]))

        def planes(i, carry, s=s, low=low):
            for u in range(UNROLL):
                carry = plane(s, low + UNROLL * i + u, carry)
            return carry

        lax.fori_loop(0, (high - low) // UNROLL, planes, carry)

    _, _, c, g = place()
    b = anchors[g]
    odd = (c + b) % 2
    for out, start in ((keep, odd), (send, 1 - odd)):
        at = (b + start) // 2
        for i in range(8):
            out[at + i] = corr[pl.ds(pl.multiple_of(32 * (start + 2 * i), 32), 32), :]


def march(*operands):
    plane = (ROWS, DEPTH)
    return pl.pallas_call(
        march_kernel,
        out_shape=[shape(16, 32, DEPTH)] * 2,
        in_specs=[SMEM] + [VMEM] * 9,
        out_specs=[VMEM] * 2,
        scratch_shapes=[
            pltpu.VMEM((STEPS, PLANES, *plane), F32),
            pltpu.VMEM((STEPS, PLANES, *plane), F32),
            pltpu.VMEM((PLANES, *plane), F32),
            pltpu.VMEM((PLANES, *plane), F32),
            pltpu.VMEM((PLANES, *plane), F32),
            pltpu.VMEM((PLANES, *plane), F32),
            pltpu.VMEM((COLS * ROWS, DEPTH), F32),
        ],
        compiler_params=params(24),
        name="march",
    )(*operands)


def halve_kernel(keep, got, s0, s1, s2, s3):
    x, _, _, _ = place()
    for d, out in enumerate((s0, s1, s2, s3)):
        at = ((x + d) % NX) * NZH
        for i in range(NZH):
            out[i] = keep[at + i] + got[at + i]


def quarter_kernel(s0, r1, r2, r3, u0, u1, u2, u3):
    _, z, _, _ = place()
    for d, out in enumerate((u0, u1, u2, u3)):
        at = (z + d) % NZH
        out[...] = (s0[at] + r1[at]) + (r2[at] + r3[at])


def last_kernel(u0, q1, q2, q3, out):
    out[...] = (u0[...] + q1[...]) + (q2[...] + q3[...])


def along(block, axis, distance):
    route = []
    for s in range(NX * NZH * NC):
        x, z, c = s // (NZH * NC), (s // NC) % NZH, s % NC
        if axis == "x":
            x = (x + distance) % NX
        elif axis == "z":
            z = (z + distance) % NZH
        else:
            c = (c + distance) % NC
        route.append((s, (x * NZH + z) * NC + c))
    return lax.ppermute(block, "shot", route)


def to_tile(block, distance):
    route = [(i, i + distance) for i in range(NT) if 0 <= i + distance < NT]
    return lax.ppermute(block, "tile", route)


def local(velocity, density, anchors, src_state, rcv_state, src_pos, wavelet, rec_pos, traces):
    plane = (ROWS, DEPTH)
    model = jnp.stack([velocity, density])[None]
    zs = [along(model, "z", d) for d in range(1, NZH)]

    own, to_prev, to_next = pl.pallas_call(
        pack_kernel,
        out_shape=[shape(4, COLS * ROWS, DEPTH), shape(13, *plane), shape(15, *plane)],
        in_specs=[VMEM, VMEM],
        out_specs=[VMEM] * 3,
        compiler_params=params(16),
        name="pack",
    )(src_state, rcv_state)

    xs = [jnp.concatenate([model, *zs])]
    xs += [along(xs[0], "x", d) for d in range(1, NX)]

    halo_next = to_tile(to_prev, -1)
    halo_prev = to_tile(to_next, 1)

    inj_src, inj_rec = pl.pallas_call(
        inject_kernel,
        out_shape=[shape(STEPS, PLANES, *plane)] * 2,
        in_specs=[SMEM] * 4,
        out_specs=[VMEM] * 2,
        compiler_params=params(16),
        name="inject",
    )(src_pos, wavelet, rec_pos, traces)

    strips = (8, 2, 4, COLS, DEPTH)
    mine, other = pl.pallas_call(
        window_kernel,
        out_shape=[shape(*strips)] * 2,
        in_specs=[SMEM] + [ANY] * 4,
        out_specs=[VMEM] * 2,
        scratch_shapes=[
            pltpu.VMEM((NX, NZH, 2, 4, COLS, DEPTH), F32),
            pltpu.SemaphoreType.DMA((NX,)),
        ],
        compiler_params=params(16),
        name="window",
    )(anchors, *xs)
    got = along(other, "core", 1)

    mb, mb_prev, mb_next = pl.pallas_call(
        model_kernel,
        out_shape=[shape(2, COLS * ROWS, DEPTH), shape(6, *plane), shape(7, *plane)],
        in_specs=[SMEM, VMEM, VMEM],
        out_specs=[VMEM] * 3,
        compiler_params=params(16),
        name="model",
    )(anchors, mine, got)
    model_next = to_tile(mb_prev, -1)
    model_prev = to_tile(mb_next, 1)

    keep, send = march(
        anchors,
        own.reshape(4, COLS, *plane),
        halo_prev,
        halo_next,
        to_next,
        mb.reshape(2, COLS, *plane),
        model_prev,
        model_next,
        inj_src,
        inj_rec,
    )

    received = along(send, "core", 1)
    parts = pl.pallas_call(
        halve_kernel,
        out_shape=[shape(NZH, 32, DEPTH)] * NX,
        in_specs=[VMEM] * 2,
        out_specs=[VMEM] * NX,
        compiler_params=params(8),
        name="halve",
    )(keep, received)
    moved = [along(parts[d], "x", d) for d in range(1, NX)]
    parts = pl.pallas_call(
        quarter_kernel,
        out_shape=[shape(32, DEPTH)] * NZH,
        in_specs=[VMEM] * NX,
        out_specs=[VMEM] * NZH,
        compiler_params=params(8),
        name="quarter",
    )(parts[0], *moved)
    moved = [along(parts[d], "z", d) for d in range(1, NZH)]
    image = pl.pallas_call(
        last_kernel,
        out_shape=shape(32, DEPTH),
        in_specs=[VMEM] * NZH,
        out_specs=VMEM,
        compiler_params=params(8),
        name="last",
    )(parts[0], *moved)
    return image.reshape(4, COLS, DEPTH)


def solution(mesh):
    return jax.shard_map(
        local,
        mesh=mesh,
        in_specs=(
            P("shot", "tile", None),
            P("shot", "tile", None),
            P(),
            P(None, "shot", "tile", None),
            P(None, "shot", "tile", None),
            P("shot", None),
            P("shot", None, None),
            P("shot", None),
            P("shot", None, None),
        ),
        out_specs=P("shot", "tile", None),
        check_vma=False,
    )
```

```python
import jax
import jax.numpy as jnp
from jax import lax
from jax.experimental import pallas as pl
from jax.experimental.pallas import tpu as pltpu
from jax.sharding import Mesh
from jax.sharding import PartitionSpec as P

STEPS = 4
UNROLL = 2
F32 = jnp.float32
ROWS = 64
COLS = 8
DEPTH = 128
PLANES = COLS + 2 * STEPS
NX, NZH, NC, NT = 4, 4, 2, 8

VMEM = pl.BlockSpec(memory_space=pltpu.VMEM)
SMEM = pl.BlockSpec(memory_space=pltpu.SMEM)
ANY = pl.BlockSpec(memory_space=pl.ANY)
HBM = pl.BlockSpec(memory_space=pltpu.HBM)


def shape(*dims):
    return jax.ShapeDtypeStruct(dims, F32)


def params(mib):
    return pltpu.CompilerParams(vmem_limit_bytes=mib * 1024 * 1024)


def place():
    c = lax.axis_index("core")
    return c, (lax.axis_index("x") * NZH + lax.axis_index("zh")) * NC + c


def first_strip(b, c):
    return (b + ((c + b) & 1)) >> 1


def pack_kernel(src_in, rcv_in, own, to_prev, to_next, src, rcv, sem):
    half = ROWS // 2
    copies = []
    for h in range(2):
        cut = slice(h * half, h * half + half)
        for f, (a, b) in enumerate(((src_in, src), (rcv_in, rcv))):
            copies.append(pltpu.make_async_copy(a.at[:, cut], b.at[:, cut], sem.at[h, f]))
            copies[-1].start()
    lane = lax.broadcasted_iota(jnp.int32, (COLS, DEPTH), 1)
    col = lax.broadcasted_iota(jnp.int32, (COLS, DEPTH), 0)

    def row(x, before):
        after = []
        for f, state in enumerate((src, rcv)):
            p, vx, vy, vz = (state[i, x] for i in range(4))
            spread = vx - before[f]
            spread += vy - jnp.where(col == 0, 0.0, pltpu.roll(vy, 1, 0))
            spread += vz - jnp.where(lane == 0, 0.0, pltpu.roll(vz, 1, 1))
            own[2 * f, pl.ds(x, COLS, stride=ROWS), :] = p
            own[2 * f + 1, pl.ds(x, COLS, stride=ROWS), :] = spread
            to_next[7 + 7 * f, pl.ds(x, 1), :] = vy[COLS - 1 :, :]
            after.append(vx)
        return tuple(after)

    before = (jnp.zeros((COLS, DEPTH), F32),) * 2
    for h in range(2):
        for copy in copies[2 * h : 2 * h + 2]:
            copy.wait()
        before = lax.fori_loop(h * half, h * half + half, row, before, unroll=8)

    def plane(f, y):
        return own[f, y * ROWS : (y + 1) * ROWS, :]

    for i, (f, y) in enumerate(
        [(0, 0), (0, 1), (0, 2), (0, 3), (1, 0), (1, 1), (1, 2)]
        + [(2, 0), (2, 1), (2, 2), (3, 0), (3, 1), (3, 2)]
    ):
        to_prev[i] = plane(f, y)
    for i, (f, y) in (
        list(enumerate([(0, 4), (0, 5), (0, 6), (0, 7), (1, 5), (1, 6), (1, 7)]))
        + list(enumerate([(2, 5), (2, 6), (2, 7), (3, 5), (3, 6), (3, 7)], 8))
    ):
        to_next[i] = plane(f, y)


def inject_kernel(src_pos, wavelet, rec_pos, traces, src_out, rec_out):
    for out in (src_out, rec_out):
        for s in range(STEPS):
            out[s, 1 : PLANES - 1] = jnp.zeros((PLANES - 2, ROWS, DEPTH), F32)
    first = lax.axis_index("tile") * COLS - STEPS
    lane = lax.broadcasted_iota(jnp.int32, (1, DEPTH), 1)
    for pos, amp, out in ((src_pos, wavelet, src_out), (rec_pos, traces, rec_out)):

        def point(k, _, pos=pos, amp=amp, out=out):
            cell = pos[0, k]
            x = cell >> 13
            y = jnp.clip(((cell >> 7) & (COLS * NT - 1)) - first, 0, PLANES - 1)
            hit = lane == (cell & (DEPTH - 1))
            old = [out[s, y, pl.ds(x, 1), :] for s in range(STEPS)]
            for s in range(STEPS):
                out[s, y, pl.ds(x, 1), :] = old[s] + jnp.where(hit, amp[s, k], 0.0)
            return 0

        lax.fori_loop(0, pos.shape[1], point, 0, unroll=8)


def window_kernel(anchors, a0, a1, a2, a3, own, other):
    x, z = lax.axis_index("x"), lax.axis_index("zh")
    c, g = place()
    for group, out in ((g, own), (g + 1 - 2 * c, other)):
        first = first_strip(anchors[group], c)
        for dx, strips in enumerate((a0, a1, a2, a3)):
            for dz in range(NZH):
                i = ((x - dx) & (NX - 1)) * NZH + ((z - dz) & (NZH - 1)) - first

                @pl.when((i >= 0) & (i < 8))
                def _(i=i, strips=strips, dz=dz, out=out):
                    vel, den = strips[dz, 0], strips[dz, 1]
                    out[i, 0] = den * vel * vel
                    out[i, 1] = 1.0 / den


def model_kernel(anchors, own, other, out, to_prev, to_next):
    c, g = place()
    odd = (c + anchors[g]) & 1
    for strips, start in ((own, odd), (other, 1 - odd)):
        for i in range(8):
            for r in range(4):
                x = 4 * (start + 2 * i) + r
                for f in range(2):
                    out[f, pl.ds(x, COLS, stride=ROWS), :] = strips[i, f, r]

    def plane(f, y):
        return out[f, y * ROWS : (y + 1) * ROWS, :]

    for i, (f, y) in enumerate([(0, 0), (0, 1), (0, 2), (1, 0), (1, 1), (1, 2)]):
        to_prev[i] = plane(f, y)
    for i, (f, y) in enumerate([(0, 5), (0, 6), (0, 7), (1, 4), (1, 5), (1, 6), (1, 7)]):
        to_next[i] = plane(f, y)


def march_kernel(
    anchors, own, prev, nxt, mine, model, model_prev, model_next, add_s, add_r,
    keep, send,
    ps, pr, ds, dr, mod, buoy, corr,
):
    tile = lax.axis_index("tile")
    inner_low, inner_high = tile > 0, tile < NT - 1

    def below(value):
        return jnp.where(inner_low, value, 0.0)

    def above(value):
        return jnp.where(inner_high, value, 0.0)

    ps[0, 0:4] = below(prev[0:4])
    ps[0, 4:12] = own[0]
    ps[0, 12:16] = above(nxt[0:4])
    pr[0, 1:4] = below(prev[8:11])
    pr[0, 4:12] = own[2]
    pr[0, 12:15] = above(nxt[7:10])
    for d, f, at, vy, after in ((ds, 0, 4, 7, 4), (dr, 1, 11, 14, 10)):
        d[1:4] = below(prev[at : at + 3])
        d[4] = own[2 * f + 1, 0] - below(prev[vy])
        d[5:12] = own[2 * f + 1, 1:8]
        d[12] = above(nxt[after] - mine[vy])
        d[13:15] = above(nxt[after + 1 : after + 3])
    mod[1:4] = below(model_prev[0:3])
    mod[4:12] = model[0]
    mod[12:15] = above(model_next[0:3])
    buoy[0:4] = below(model_prev[3:7])
    buoy[4:12] = model[1]
    buoy[12:15] = above(model_next[3:6])

    keep[...] = jnp.zeros(keep.shape, F32)
    send[...] = jnp.zeros(send.shape, F32)

    lane = lax.broadcasted_iota(jnp.int32, (8, DEPTH), 1)
    row = lax.broadcasted_iota(jnp.int32, (8, DEPTH), 0)
    first_lane, last_lane, first_row, last_row = lane == 0, lane == DEPTH - 1, row == 0, row == 7
    blocks = range(ROWS // 8)
    zero = jnp.zeros((8, DEPTH), F32)

    def get(ref, *at):
        return [ref[(*at, slice(8 * v, 8 * v + 8))] for v in blocks]

    def spread_of(p, after, before, b):
        down = [pltpu.roll(p[v], 7, 0) for v in blocks] + [zero]
        flux_y = [b[v] * (after[v] - p[v]) for v in blocks]
        out, last = [], zero
        for v in blocks:
            flux_x = b[v] * (jnp.where(last_row, down[v + 1], down[v]) - p[v])
            flux_z = b[v] * (jnp.where(last_lane, 0.0, pltpu.roll(p[v], DEPTH - 1, 1)) - p[v])
            turned = pltpu.roll(flux_x, 1, 0)
            spread = (flux_x - jnp.where(first_row, last, turned)) + (flux_y[v] - before[v])
            spread += flux_z - jnp.where(first_lane, 0.0, pltpu.roll(flux_z, 1, 1))
            last = turned
            out.append(spread)
        return out, flux_y

    def plane(s, y, carry):
        m, b = get(mod, y), get(buoy, y)
        fields = ((ps, ds, add_s, s), (pr, dr, add_r, STEPS - s)) if s else ((ps, ds, add_s, 0),)
        new, ends = [], []
        for (p_all, d_all, add, amp), (p, before) in zip(fields, carry):
            after = get(p_all, s, y + 1)
            spread, flux = spread_of(p, after, before, b)
            ends.append((after, flux))
            out = []
            for v in blocks:
                cut = slice(8 * v, 8 * v + 8)
                d = d_all[y, cut] - spread[v]
                out.append(p[v] + add[amp, y, cut] - m[v] * d)
                if s < STEPS - 1:
                    d_all[y, cut] = d
                    p_all[s + 1, y, cut] = out[v]
            new.append(out)
        if s == 0:
            for v in blocks:
                cut = slice(8 * v, 8 * v + 8)
                pr[1, y, cut] = pr[0, y, cut] - m[v] * dr[y, cut]
        if s == STEPS - 1:
            for v in blocks:
                cut = slice(8 * v, 8 * v + 8)
                image = new[0][v] * (pr[1, y, cut] + add_r[3, y, cut])
                image += ps[3, y, cut] * (pr[2, y, cut] + add_r[2, y, cut])
                image += ps[2, y, cut] * (pr[3, y, cut] + add_r[1, y, cut])
                image += ps[1, y, cut] * (new[1][v] + add_r[0, y, cut])
                corr[pl.ds(8 * COLS * v + y - STEPS, 8, stride=COLS), :] = image / STEPS
        return ends

    for s in range(STEPS):
        low, high = s + 1, 15 - s
        carry = []
        for p_all in (ps, pr) if s else (ps,):
            here, before, b = get(p_all, s, low), get(p_all, s, low - 1), get(buoy, low - 1)
            carry.append((here, [b[v] * (here[v] - before[v]) for v in blocks]))

        def planes(i, carry, s=s, low=low):
            for u in range(UNROLL):
                carry = plane(s, low + UNROLL * i + u, carry)
            return carry

        lax.fori_loop(0, (high - low) // UNROLL, planes, carry)

    c, g = place()
    odd = (c + anchors[g]) & 1
    for out, start in ((keep, odd), (send, 1 - odd)):
        at = (anchors[g] + start) >> 1
        for i in range(8):
            out[at + i] = corr[pl.ds(pl.multiple_of(32 * (start + 2 * i), 32), 32), :]


def march(*operands):
    plane = (ROWS, DEPTH)
    return pl.pallas_call(
        march_kernel,
        out_shape=[shape(16, 32, DEPTH)] * 2,
        in_specs=[SMEM] + [VMEM] * 9,
        out_specs=[VMEM] * 2,
        scratch_shapes=[
            pltpu.VMEM((STEPS, PLANES, *plane), F32),
            pltpu.VMEM((STEPS, PLANES, *plane), F32),
            pltpu.VMEM((PLANES, *plane), F32),
            pltpu.VMEM((PLANES, *plane), F32),
            pltpu.VMEM((PLANES, *plane), F32),
            pltpu.VMEM((PLANES, *plane), F32),
            pltpu.VMEM((COLS * ROWS, DEPTH), F32),
        ],
        compiler_params=params(10),
        name="march",
    )(*operands)


def halve_kernel(keep, got, s0, s1, s2, s3):
    x = lax.axis_index("x")
    for d, out in enumerate((s0, s1, s2, s3)):
        at = ((x + d) & (NX - 1)) * NZH
        for i in range(NZH):
            out[i] = keep[at + i] + got[at + i]


def quarter_kernel(s0, r1, r2, r3, u0, u1, u2, u3):
    z = lax.axis_index("zh")
    for d, out in enumerate((u0, u1, u2, u3)):
        at = (z + d) & (NZH - 1)
        out[...] = (s0[at] + r1[at]) + (r2[at] + r3[at])


def last_kernel(u0, q1, q2, q3, out):
    out[...] = (u0[...] + q1[...]) + (q2[...] + q3[...])


def other_core(block):
    return lax.ppermute(block, "core", [(0, 1), (1, 0)])


def to_tile(block, distance):
    return lax.ppermute(block, "tile", [(i, (i + distance) % NT) for i in range(NT)])


def along(block, axis, distance):
    return lax.ppermute(block, axis, [(i, (i + distance) % 4) for i in range(4)])


def local(velocity, density, anchors, src_state, rcv_state, src_pos, wavelet, rec_pos, traces):
    plane = (ROWS, DEPTH)
    strip = jnp.stack([velocity, density])[None]
    zs = [along(strip, "zh", d) for d in range(1, NZH)]

    own, to_prev, to_next = pl.pallas_call(
        pack_kernel,
        out_shape=[shape(4, COLS * ROWS, DEPTH), shape(13, *plane), shape(15, *plane)],
        in_specs=[HBM, HBM],
        out_specs=[VMEM] * 3,
        scratch_shapes=[
            pltpu.VMEM((4, ROWS, COLS, DEPTH), F32),
            pltpu.VMEM((4, ROWS, COLS, DEPTH), F32),
            pltpu.SemaphoreType.DMA((2, 2)),
        ],
        compiler_params=params(8),
        name="pack",
    )(*(pltpu.with_memory_space_constraint(state, pltpu.HBM) for state in (src_state, rcv_state)))
    *zs, own, to_prev, to_next = lax.optimization_barrier((*zs, own, to_prev, to_next))

    xs = [jnp.concatenate([strip, *zs])]
    xs += [along(xs[0], "x", d) for d in range(1, NX)]

    halo_next = to_tile(to_prev, -1)
    halo_prev = to_tile(to_next, 1)

    inj_src, inj_rec = pl.pallas_call(
        inject_kernel,
        out_shape=[shape(STEPS, PLANES, *plane)] * 2,
        in_specs=[SMEM] * 4,
        out_specs=[VMEM] * 2,
        compiler_params=params(2),
        name="inject",
    )(src_pos, wavelet[0].T, rec_pos, traces[0].T)

    mine, other = pl.pallas_call(
        window_kernel,
        out_shape=[shape(8, *strip.shape[1:])] * 2,
        in_specs=[SMEM] + [VMEM] * 4,
        out_specs=[VMEM] * 2,
        compiler_params=params(2),
        name="window",
    )(anchors, *xs)
    got = other_core(other)
    got, halo_prev, halo_next = lax.optimization_barrier((got, halo_prev, halo_next))

    mb, mb_prev, mb_next = pl.pallas_call(
        model_kernel,
        out_shape=[shape(2, COLS * ROWS, DEPTH), shape(6, *plane), shape(7, *plane)],
        in_specs=[SMEM, VMEM, VMEM],
        out_specs=[VMEM] * 3,
        compiler_params=params(2),
        name="model",
    )(anchors, mine, got)
    model_next = to_tile(mb_prev, -1)
    model_prev = to_tile(mb_next, 1)

    keep, send = march(
        anchors,
        own.reshape(4, COLS, *plane),
        halo_prev,
        halo_next,
        to_next,
        mb.reshape(2, COLS, *plane),
        model_prev,
        model_next,
        inj_src,
        inj_rec,
    )

    parts = pl.pallas_call(
        halve_kernel,
        out_shape=[shape(NZH, 32, DEPTH)] * NX,
        in_specs=[VMEM, VMEM],
        out_specs=[VMEM] * NX,
        compiler_params=params(2),
        name="halve",
    )(keep, other_core(send))
    moved = [along(parts[d], "x", d) for d in range(1, NX)]
    parts = pl.pallas_call(
        quarter_kernel,
        out_shape=[shape(32, DEPTH)] * NZH,
        in_specs=[VMEM] * NX,
        out_specs=[VMEM] * NZH,
        compiler_params=params(2),
        name="quarter",
    )(parts[0], *moved)
    moved = [along(parts[d], "zh", d) for d in range(1, NZH)]
    image = pl.pallas_call(
        last_kernel,
        out_shape=shape(32, DEPTH),
        in_specs=[VMEM] * NZH,
        out_specs=VMEM,
        compiler_params=params(2),
        name="last",
    )(parts[0], *moved)
    return image.reshape(velocity.shape)


def solution(mesh):
    shot = ("x", "zh", "core")
    return jax.shard_map(
        local,
        mesh=Mesh(mesh.devices.reshape(NX, NZH, NC, NT), (*shot, "tile")),
        in_specs=(
            P(shot, "tile", None),
            P(shot, "tile", None),
            P(),
            P(None, shot, "tile", None),
            P(None, shot, "tile", None),
            P(shot, None),
            P(shot, None, None),
            P(shot, None),
            P(shot, None, None),
        ),
        out_specs=P(shot, "tile", None),
        check_vma=False,
    )
```

```python
import jax
import jax.numpy as jnp
from jax import lax
from jax.experimental import pallas as pl
from jax.experimental.pallas import tpu as pltpu
from jax.sharding import Mesh
from jax.sharding import PartitionSpec as P

STEPS = 4
UNROLL = 2
GATHER, SCATTER = (3, 1, 2), (2, 1, 3)
F32 = jnp.float32
ROWS = 64
COLS = 8
DEPTH = 128
PLANES = COLS + 2 * STEPS
NX, NZH, NC, NT = 4, 4, 2, 8

VMEM = pl.BlockSpec(memory_space=pltpu.VMEM)
SMEM = pl.BlockSpec(memory_space=pltpu.SMEM)
ANY = pl.BlockSpec(memory_space=pl.ANY)
HBM = pl.BlockSpec(memory_space=pltpu.HBM)


def shape(*dims):
    return jax.ShapeDtypeStruct(dims, F32)


def params(mib):
    return pltpu.CompilerParams(vmem_limit_bytes=mib * 1024 * 1024)


def place():
    c = lax.axis_index("core")
    return c, (lax.axis_index("x") * NZH + lax.axis_index("zh")) * NC + c


def first_strip(b, c):
    return (b + ((c + b) & 1)) >> 1


def pack_kernel(src_in, rcv_in, own, to_prev, to_next, src, rcv, sem):
    half = ROWS // 2
    copies = []
    for h in range(2):
        cut = slice(h * half, h * half + half)
        for f, (a, b) in enumerate(((src_in, src), (rcv_in, rcv))):
            copies.append(pltpu.make_async_copy(a.at[:, cut], b.at[:, cut], sem.at[h, f]))
            copies[-1].start()
    lane = lax.broadcasted_iota(jnp.int32, (COLS, DEPTH), 1)
    col = lax.broadcasted_iota(jnp.int32, (COLS, DEPTH), 0)

    def row(x, before):
        after = []
        for f, state in enumerate((src, rcv)):
            p, vx, vy, vz = (state[i, x] for i in range(4))
            spread = vx - before[f]
            spread += vy - jnp.where(col == 0, 0.0, pltpu.roll(vy, 1, 0))
            spread += vz - jnp.where(lane == 0, 0.0, pltpu.roll(vz, 1, 1))
            own[2 * f, pl.ds(x, COLS, stride=ROWS), :] = p
            own[2 * f + 1, pl.ds(x, COLS, stride=ROWS), :] = spread
            to_next[7 + 7 * f, pl.ds(x, 1), :] = vy[COLS - 1 :, :]
            after.append(vx)
        return tuple(after)

    before = (jnp.zeros((COLS, DEPTH), F32),) * 2
    for h in range(2):
        for copy in copies[2 * h : 2 * h + 2]:
            copy.wait()
        before = lax.fori_loop(h * half, h * half + half, row, before, unroll=8)

    def plane(f, y):
        return own[f, y * ROWS : (y + 1) * ROWS, :]

    for i, (f, y) in enumerate(
        [(0, 0), (0, 1), (0, 2), (0, 3), (1, 0), (1, 1), (1, 2)]
        + [(2, 0), (2, 1), (2, 2), (3, 0), (3, 1), (3, 2)]
    ):
        to_prev[i] = plane(f, y)
    for i, (f, y) in (
        list(enumerate([(0, 4), (0, 5), (0, 6), (0, 7), (1, 5), (1, 6), (1, 7)]))
        + list(enumerate([(2, 5), (2, 6), (2, 7), (3, 5), (3, 6), (3, 7)], 8))
    ):
        to_next[i] = plane(f, y)


def inject_kernel(src_pos, wavelet, rec_pos, traces, src_out, rec_out):
    for out in (src_out, rec_out):
        for s in range(STEPS):
            out[s, 1 : PLANES - 1] = jnp.zeros((PLANES - 2, ROWS, DEPTH), F32)
    first = lax.axis_index("tile") * COLS - STEPS
    lane = lax.broadcasted_iota(jnp.int32, (1, DEPTH), 1)
    for pos, amp, out in ((src_pos, wavelet, src_out), (rec_pos, traces, rec_out)):

        def point(k, _, pos=pos, amp=amp, out=out):
            cell = pos[0, k]
            x = cell >> 13
            y = jnp.clip(((cell >> 7) & (COLS * NT - 1)) - first, 0, PLANES - 1)
            hit = lane == (cell & (DEPTH - 1))
            old = [out[s, y, pl.ds(x, 1), :] for s in range(STEPS)]
            for s in range(STEPS):
                out[s, y, pl.ds(x, 1), :] = old[s] + jnp.where(hit, amp[s, k], 0.0)
            return 0

        lax.fori_loop(0, pos.shape[1], point, 0, unroll=8)


def window_kernel(anchors, a0, a1, a2, a3, own_m, own_b, other_m, other_b):
    x, z = lax.axis_index("x"), lax.axis_index("zh")
    c, g = place()
    for group, out in ((g, (own_m, own_b)), (g + 1 - 2 * c, (other_m, other_b))):
        first = first_strip(anchors[group], c)
        for dx, strips in zip((0, *GATHER), (a0, a1, a2, a3)):
            for dz, at in zip((0, *GATHER), range(NZH)):
                i = ((x - dx) & (NX - 1)) * NZH + ((z - dz) & (NZH - 1)) - first

                @pl.when((i >= 0) & (i < 8))
                def _(i=i, strips=strips, at=at, out=out):
                    vel, den = strips[at, 0], strips[at, 1]
                    out[0][i] = den * vel * vel
                    out[1][i] = 1.0 / den


def model_kernel(anchors, own_m, own_b, other_m, other_b, out, to_prev, to_next):
    c, g = place()
    odd = (c + anchors[g]) & 1
    for strips, start in (((own_m, own_b), odd), ((other_m, other_b), 1 - odd)):
        for i in range(8):
            for r in range(4):
                x = 4 * (start + 2 * i) + r
                for f in range(2):
                    out[f, pl.ds(x, COLS, stride=ROWS), :] = strips[f][i, r]

    def plane(f, y):
        return out[f, y * ROWS : (y + 1) * ROWS, :]

    for i, (f, y) in enumerate([(0, 0), (0, 1), (0, 2), (1, 0), (1, 1), (1, 2)]):
        to_prev[i] = plane(f, y)
    for i, (f, y) in enumerate([(0, 5), (0, 6), (0, 7), (1, 4), (1, 5), (1, 6), (1, 7)]):
        to_next[i] = plane(f, y)


def march_kernel(
    anchors, own, prev, nxt, mine, model, model_prev, model_next, add_s, add_r,
    keep, send,
    ps, pr, ds, dr, mod, buoy, corr,
):
    tile = lax.axis_index("tile")
    inner_low, inner_high = tile > 0, tile < NT - 1

    def below(value):
        return jnp.where(inner_low, value, 0.0)

    def above(value):
        return jnp.where(inner_high, value, 0.0)

    ps[0, 0:4] = below(prev[0:4])
    ps[0, 4:12] = own[0]
    ps[0, 12:16] = above(nxt[0:4])
    pr[0, 1:4] = below(prev[8:11])
    pr[0, 4:12] = own[2]
    pr[0, 12:15] = above(nxt[7:10])
    for d, f, at, vy, after in ((ds, 0, 4, 7, 4), (dr, 1, 11, 14, 10)):
        d[1:4] = below(prev[at : at + 3])
        d[4] = own[2 * f + 1, 0] - below(prev[vy])
        d[5:12] = own[2 * f + 1, 1:8]
        d[12] = above(nxt[after] - mine[vy])
        d[13:15] = above(nxt[after + 1 : after + 3])
    mod[1:4] = below(model_prev[0:3])
    mod[4:12] = model[0]
    mod[12:15] = above(model_next[0:3])
    buoy[0:4] = below(model_prev[3:7])
    buoy[4:12] = model[1]
    buoy[12:15] = above(model_next[3:6])

    keep[...] = jnp.zeros(keep.shape, F32)
    send[...] = jnp.zeros(send.shape, F32)

    lane = lax.broadcasted_iota(jnp.int32, (8, DEPTH), 1)
    row = lax.broadcasted_iota(jnp.int32, (8, DEPTH), 0)
    first_lane, last_lane, first_row, last_row = lane == 0, lane == DEPTH - 1, row == 0, row == 7
    blocks = range(ROWS // 8)
    zero = jnp.zeros((8, DEPTH), F32)

    def get(ref, *at):
        return [ref[(*at, slice(8 * v, 8 * v + 8))] for v in blocks]

    def spread_of(p, after, before, b):
        down = [pltpu.roll(p[v], 7, 0) for v in blocks] + [zero]
        flux_y = [b[v] * (after[v] - p[v]) for v in blocks]
        out, last = [], zero
        for v in blocks:
            flux_x = b[v] * (jnp.where(last_row, down[v + 1], down[v]) - p[v])
            flux_z = b[v] * (jnp.where(last_lane, 0.0, pltpu.roll(p[v], DEPTH - 1, 1)) - p[v])
            turned = pltpu.roll(flux_x, 1, 0)
            spread = (flux_x - jnp.where(first_row, last, turned)) + (flux_y[v] - before[v])
            spread += flux_z - jnp.where(first_lane, 0.0, pltpu.roll(flux_z, 1, 1))
            last = turned
            out.append(spread)
        return out, flux_y

    def plane(s, y, carry):
        m, b = get(mod, y), get(buoy, y)
        fields = ((ps, ds, add_s, s), (pr, dr, add_r, STEPS - s)) if s else ((ps, ds, add_s, 0),)
        new, ends = [], []
        for (p_all, d_all, add, amp), (p, before) in zip(fields, carry):
            after = get(p_all, s, y + 1)
            spread, flux = spread_of(p, after, before, b)
            ends.append((after, flux))
            out = []
            for v in blocks:
                cut = slice(8 * v, 8 * v + 8)
                d = d_all[y, cut] - spread[v]
                out.append(p[v] + add[amp, y, cut] - m[v] * d)
                if s < STEPS - 1:
                    d_all[y, cut] = d
                    p_all[s + 1, y, cut] = out[v]
            new.append(out)
        if s == 0:
            for v in blocks:
                cut = slice(8 * v, 8 * v + 8)
                pr[1, y, cut] = pr[0, y, cut] - m[v] * dr[y, cut]
        if s == STEPS - 1:
            for v in blocks:
                cut = slice(8 * v, 8 * v + 8)
                image = new[0][v] * (pr[1, y, cut] + add_r[3, y, cut])
                image += ps[3, y, cut] * (pr[2, y, cut] + add_r[2, y, cut])
                image += ps[2, y, cut] * (pr[3, y, cut] + add_r[1, y, cut])
                image += ps[1, y, cut] * (new[1][v] + add_r[0, y, cut])
                corr[pl.ds(8 * COLS * v + y - STEPS, 8, stride=COLS), :] = image / STEPS
        return ends

    for s in range(STEPS):
        low, high = s + 1, 15 - s
        carry = []
        for p_all in (ps, pr) if s else (ps,):
            here, before, b = get(p_all, s, low), get(p_all, s, low - 1), get(buoy, low - 1)
            carry.append((here, [b[v] * (here[v] - before[v]) for v in blocks]))

        def planes(i, carry, s=s, low=low):
            for u in range(UNROLL):
                carry = plane(s, low + UNROLL * i + u, carry)
            return carry

        lax.fori_loop(0, (high - low) // UNROLL, planes, carry)

    c, g = place()
    odd = (c + anchors[g]) & 1
    for out, start in ((keep, odd), (send, 1 - odd)):
        at = (anchors[g] + start) >> 1
        for i in range(8):
            out[at + i] = corr[pl.ds(pl.multiple_of(32 * (start + 2 * i), 32), 32), :]


def march(*operands):
    plane = (ROWS, DEPTH)
    return pl.pallas_call(
        march_kernel,
        out_shape=[shape(16, 32, DEPTH)] * 2,
        in_specs=[SMEM] + [VMEM] * 9,
        out_specs=[VMEM] * 2,
        scratch_shapes=[
            pltpu.VMEM((STEPS, PLANES, *plane), F32),
            pltpu.VMEM((STEPS, PLANES, *plane), F32),
            pltpu.VMEM((PLANES, *plane), F32),
            pltpu.VMEM((PLANES, *plane), F32),
            pltpu.VMEM((PLANES, *plane), F32),
            pltpu.VMEM((PLANES, *plane), F32),
            pltpu.VMEM((COLS * ROWS, DEPTH), F32),
        ],
        compiler_params=params(10),
        name="march",
    )(*operands)


def halve_kernel(keep, got, s0, s1, s2, s3):
    x = lax.axis_index("x")
    for d, out in enumerate((s0, s1, s2, s3)):
        at = ((x + d) & (NX - 1)) * NZH
        for i in range(NZH):
            out[i] = keep[at + i] + got[at + i]


def quarter_kernel(s0, r1, r2, r3, u0, u1, u2, u3):
    z = lax.axis_index("zh")
    for d, out in enumerate((u0, u1, u2, u3)):
        at = (z + d) & (NZH - 1)
        out[...] = (s0[at] + r1[at]) + (r2[at] + r3[at])


def last_kernel(u0, q1, q2, q3, out):
    out[...] = (u0[...] + q1[...]) + (q2[...] + q3[...])


def other_core(block):
    return lax.ppermute(block, "core", [(0, 1), (1, 0)])


def to_tile(block, distance):
    return lax.ppermute(block, "tile", [(i, (i + distance) % NT) for i in range(NT)])


def along(blocks, axis, order):
    return [lax.ppermute(blocks[d - 1], axis, [(i, (i + d) % 4) for i in range(4)]) for d in order]


def local(velocity, density, anchors, src_state, rcv_state, src_pos, wavelet, rec_pos, traces):
    plane = (ROWS, DEPTH)
    strip = jnp.stack([velocity, density])[None]
    zs = along([strip] * 3, "zh", GATHER)

    own, to_prev, to_next = pl.pallas_call(
        pack_kernel,
        out_shape=[shape(4, COLS * ROWS, DEPTH), shape(13, *plane), shape(15, *plane)],
        in_specs=[HBM, HBM],
        out_specs=[VMEM] * 3,
        scratch_shapes=[
            pltpu.VMEM((4, ROWS, COLS, DEPTH), F32),
            pltpu.VMEM((4, ROWS, COLS, DEPTH), F32),
            pltpu.SemaphoreType.DMA((2, 2)),
        ],
        compiler_params=params(8),
        name="pack",
    )(*(pltpu.with_memory_space_constraint(state, pltpu.HBM) for state in (src_state, rcv_state)))
    *zs, own, to_prev, to_next = lax.optimization_barrier((*zs, own, to_prev, to_next))

    xs = [jnp.concatenate([strip, *zs])]
    xs += along([xs[0]] * 3, "x", GATHER)

    halo_next = to_tile(to_prev, -1)
    halo_prev = to_tile(to_next, 1)

    inj_src, inj_rec = pl.pallas_call(
        inject_kernel,
        out_shape=[shape(STEPS, PLANES, *plane)] * 2,
        in_specs=[SMEM] * 4,
        out_specs=[VMEM] * 2,
        compiler_params=params(2),
        name="inject",
    )(src_pos, wavelet[0].T, rec_pos, traces[0].T)

    *mine, other_m, other_b = pl.pallas_call(
        window_kernel,
        out_shape=[shape(8, *strip.shape[2:])] * 4,
        in_specs=[SMEM] + [VMEM] * 4,
        out_specs=[VMEM] * 4,
        compiler_params=params(2),
        name="window",
    )(anchors, *xs)
    got = [other_core(o) for o in (other_m, other_b)]

    mb, mb_prev, mb_next = pl.pallas_call(
        model_kernel,
        out_shape=[shape(2, COLS * ROWS, DEPTH), shape(6, *plane), shape(7, *plane)],
        in_specs=[SMEM] + [VMEM] * 4,
        out_specs=[VMEM] * 3,
        compiler_params=params(2),
        name="model",
    )(anchors, *mine, *got)
    model_next = to_tile(mb_prev, -1)
    model_prev = to_tile(mb_next, 1)

    keep, send = march(
        anchors,
        own.reshape(4, COLS, *plane),
        halo_prev,
        halo_next,
        to_next,
        mb.reshape(2, COLS, *plane),
        model_prev,
        model_next,
        inj_src,
        inj_rec,
    )

    parts = pl.pallas_call(
        halve_kernel,
        out_shape=[shape(NZH, 32, DEPTH)] * NX,
        in_specs=[VMEM, VMEM],
        out_specs=[VMEM] * NX,
        compiler_params=params(2),
        name="halve",
    )(keep, other_core(send))
    moved = along(parts[1:], "x", SCATTER)
    parts = pl.pallas_call(
        quarter_kernel,
        out_shape=[shape(32, DEPTH)] * NZH,
        in_specs=[VMEM] * NX,
        out_specs=[VMEM] * NZH,
        compiler_params=params(2),
        name="quarter",
    )(parts[0], *moved)
    moved = along(parts[1:], "zh", SCATTER)
    image = pl.pallas_call(
        last_kernel,
        out_shape=shape(32, DEPTH),
        in_specs=[VMEM] * NZH,
        out_specs=VMEM,
        compiler_params=params(2),
        name="last",
    )(parts[0], *moved)
    return image.reshape(velocity.shape)


def solution(mesh):
    shot = ("x", "zh", "core")
    return jax.shard_map(
        local,
        mesh=Mesh(mesh.devices.reshape(NX, NZH, NC, NT), (*shot, "tile")),
        in_specs=(
            P(shot, "tile", None),
            P(shot, "tile", None),
            P(),
            P(None, shot, "tile", None),
            P(None, shot, "tile", None),
            P(shot, None),
            P(shot, None, None),
            P(shot, None),
            P(shot, None, None),
        ),
        out_specs=P(shot, "tile", None),
        check_vma=False,
    )
```

```python
import jax
import jax.numpy as jnp
from jax import lax
from jax.experimental import pallas as pl
from jax.experimental.pallas import tpu as pltpu
from jax.sharding import Mesh
from jax.sharding import PartitionSpec as P

STEPS = 4
INLINE = 1
COST = None
GATHER, SCATTER = (3, 1, 2), (2, 1, 3)
F32 = jnp.float32
ROWS = 64
COLS = 8
DEPTH = 128
PLANES = COLS + 2 * STEPS
NX, NZH, NC, NT = 4, 4, 2, 8

VMEM = pl.BlockSpec(memory_space=pltpu.VMEM)
SMEM = pl.BlockSpec(memory_space=pltpu.SMEM)
ANY = pl.BlockSpec(memory_space=pl.ANY)
HBM = pl.BlockSpec(memory_space=pltpu.HBM)


def shape(*dims):
    return jax.ShapeDtypeStruct(dims, F32)


def params(mib):
    return pltpu.CompilerParams(vmem_limit_bytes=mib * 1024 * 1024)


def place():
    c = lax.axis_index("core")
    return c, (lax.axis_index("x") * NZH + lax.axis_index("zh")) * NC + c


def first_strip(b, c):
    return (b + ((c + b) & 1)) >> 1


def pack_kernel(src_in, rcv_in, anchors_in, own, to_prev, to_next, anchors, src, rcv, sem, anchors_sem):
    held = pltpu.make_async_copy(anchors_in, anchors, anchors_sem)
    held.start()
    half = ROWS // 2
    copies = []
    for h in range(2):
        cut = slice(h * half, h * half + half)
        for f, (a, b) in enumerate(((src_in, src), (rcv_in, rcv))):
            copies.append(pltpu.make_async_copy(a.at[:, cut], b.at[:, cut], sem.at[h, f]))
            copies[-1].start()
    lane = lax.broadcasted_iota(jnp.int32, (COLS, DEPTH), 1)
    col = lax.broadcasted_iota(jnp.int32, (COLS, DEPTH), 0)

    def row(x, before):
        after = []
        for f, state in enumerate((src, rcv)):
            p, vx, vy, vz = (state[i, x] for i in range(4))
            spread = vx - before[f]
            spread += vy - jnp.where(col == 0, 0.0, pltpu.roll(vy, 1, 0))
            spread += vz - jnp.where(lane == 0, 0.0, pltpu.roll(vz, 1, 1))
            own[2 * f, pl.ds(x, COLS, stride=ROWS), :] = p
            own[2 * f + 1, pl.ds(x, COLS, stride=ROWS), :] = spread
            to_next[7 + 7 * f, pl.ds(x, 1), :] = vy[COLS - 1 :, :]
            after.append(vx)
        return tuple(after)

    before = (jnp.zeros((COLS, DEPTH), F32),) * 2
    for h in range(2):
        for copy in copies[2 * h : 2 * h + 2]:
            copy.wait()
        before = lax.fori_loop(h * half, h * half + half, row, before, unroll=8)

    held.wait()

    def plane(f, y):
        return own[f, y * ROWS : (y + 1) * ROWS, :]

    for i, (f, y) in enumerate(
        [(0, 0), (0, 1), (0, 2), (0, 3), (1, 0), (1, 1), (1, 2)]
        + [(2, 0), (2, 1), (2, 2), (3, 0), (3, 1), (3, 2)]
    ):
        to_prev[i] = plane(f, y)
    for i, (f, y) in (
        list(enumerate([(0, 4), (0, 5), (0, 6), (0, 7), (1, 5), (1, 6), (1, 7)]))
        + list(enumerate([(2, 5), (2, 6), (2, 7), (3, 5), (3, 6), (3, 7)], 8))
    ):
        to_next[i] = plane(f, y)


def inject_kernel(src_pos, wavelet, rec_pos, traces, src_out, rec_out):
    for out in (src_out, rec_out):
        for s in range(STEPS):
            out[s, 1 : PLANES - 1] = jnp.zeros((PLANES - 2, ROWS, DEPTH), F32)
    first = lax.axis_index("tile") * COLS - STEPS
    lane = lax.broadcasted_iota(jnp.int32, (1, DEPTH), 1)
    for pos, amp, out in ((src_pos, wavelet, src_out), (rec_pos, traces, rec_out)):

        def point(k, _, pos=pos, amp=amp, out=out):
            cell = pos[0, k]
            x = cell >> 13
            y = jnp.clip(((cell >> 7) & (COLS * NT - 1)) - first, 0, PLANES - 1)
            hit = lane == (cell & (DEPTH - 1))
            old = [out[s, y, pl.ds(x, 1), :] for s in range(STEPS)]
            for s in range(STEPS):
                out[s, y, pl.ds(x, 1), :] = old[s] + jnp.where(hit, amp[s, k], 0.0)
            return 0

        lax.fori_loop(0, pos.shape[1], point, 0, unroll=8)


def window_kernel(anchors, a0, a1, a2, a3, own_m, own_b, other_m, other_b):
    x, z = lax.axis_index("x"), lax.axis_index("zh")
    c, g = place()
    for group, out in ((g, (own_m, own_b)), (g + 1 - 2 * c, (other_m, other_b))):
        first = first_strip(anchors[group], c)
        for dx, strips in zip((0, *GATHER), (a0, a1, a2, a3)):
            for dz, at in zip((0, *GATHER), range(NZH)):
                i = ((x - dx) & (NX - 1)) * NZH + ((z - dz) & (NZH - 1)) - first

                @pl.when((i >= 0) & (i < 8))
                def _(i=i, strips=strips, at=at, out=out):
                    vel, den = strips[at, 0], strips[at, 1]
                    out[0][i] = den * vel * vel
                    out[1][i] = 1.0 / den


def model_kernel(anchors, own_m, own_b, other_m, other_b, out, to_prev, to_next):
    c, g = place()
    odd = (c + anchors[g]) & 1
    for strips, start in (((own_m, own_b), odd), ((other_m, other_b), 1 - odd)):
        for i in range(8):
            for r in range(4):
                x = 4 * (start + 2 * i) + r
                for f in range(2):
                    out[f, pl.ds(x, COLS, stride=ROWS), :] = strips[f][i, r]

    def plane(f, y):
        return out[f, y * ROWS : (y + 1) * ROWS, :]

    for i, (f, y) in enumerate([(0, 0), (0, 1), (0, 2), (1, 0), (1, 1), (1, 2)]):
        to_prev[i] = plane(f, y)
    for i, (f, y) in enumerate([(0, 5), (0, 6), (0, 7), (1, 4), (1, 5), (1, 6), (1, 7)]):
        to_next[i] = plane(f, y)


def inner_tile():
    tile = lax.axis_index("tile")
    low, high = tile > 0, tile < NT - 1
    return (lambda value: jnp.where(low, value, 0.0)), (lambda value: jnp.where(high, value, 0.0))


def stepper(ps, pr, ds, dr, mod, buoy, add_s, add_r):
    lane = lax.broadcasted_iota(jnp.int32, (8, DEPTH), 1)
    row = lax.broadcasted_iota(jnp.int32, (8, DEPTH), 0)
    first_lane, last_lane, first_row, last_row = lane == 0, lane == DEPTH - 1, row == 0, row == 7
    blocks = range(ROWS // 8)
    zero = jnp.zeros((8, DEPTH), F32)
    fields = ((ps, ds, add_s, lambda s: s), (pr, dr, add_r, lambda s: STEPS - s))

    def get(ref, *at):
        return [ref[(*at, slice(8 * v, 8 * v + 8))] for v in blocks]

    def spread_of(p, after, before, b):
        down = [pltpu.roll(p[v], 7, 0) for v in blocks] + [zero]
        flux_y = [b[v] * (after[v] - p[v]) for v in blocks]
        out, last = [], zero
        for v in blocks:
            flux_x = b[v] * (jnp.where(last_row, down[v + 1], down[v]) - p[v])
            flux_z = b[v] * (jnp.where(last_lane, 0.0, pltpu.roll(p[v], DEPTH - 1, 1)) - p[v])
            turned = pltpu.roll(flux_x, 1, 0)
            spread = (flux_x - jnp.where(first_row, last, turned)) + (flux_y[v] - before[v])
            spread += flux_z - jnp.where(first_lane, 0.0, pltpu.roll(flux_z, 1, 1))
            last = turned
            out.append(spread)
        return out, flux_y

    def plane(s, y, wanted, carry):
        m, b = get(mod, y), get(buoy, y)
        ends = []
        for f, (p, before) in zip(wanted, carry):
            p_all, d_all, add, amp = fields[f]
            after = get(p_all, s, y + 1)
            spread, flux = spread_of(p, after, before, b)
            ends.append((after, flux))
            for v in blocks:
                cut = slice(8 * v, 8 * v + 8)
                d = d_all[y, cut] - spread[v]
                p_all[s + 1, y, cut] = p[v] + add[amp(s), y, cut] - m[v] * d
                if s < STEPS - 1:
                    d_all[y, cut] = d
        return ends

    def run(s, groups, count, inline=0):
        carry = []
        for y, wanted in groups:
            b, part = get(buoy, y - 1), []
            for f in wanted:
                here, before = get(fields[f][0], s, y), get(fields[f][0], s, y - 1)
                part.append((here, [b[v] * (here[v] - before[v]) for v in blocks]))
            carry.append(part)

        def planes(i, carry):
            return [plane(s, y + i, wanted, part) for (y, wanted), part in zip(groups, carry)]

        if inline:
            for i in range(count):
                carry = planes(i, carry)
        else:
            lax.fori_loop(0, count, planes, carry)

    def first(low, high):
        for y in range(low, high):
            for v in blocks:
                cut = slice(8 * v, 8 * v + 8)
                pr[1, y, cut] = pr[0, y, cut] - mod[y, cut] * dr[y, cut]

    return run, first


def inner_kernel(own, prev, nxt, mine, model, add_s, add_r, ps, pr, ds, dr, mod, buoy):
    below, above = inner_tile()
    mod[4:12] = model[0]
    buoy[4:12] = model[1]
    ps[0, 0:4] = below(prev[0:4])
    ps[0, 4:12] = own[0]
    ps[0, 12:16] = above(nxt[0:4])
    pr[0, 1:4] = below(prev[8:11])
    pr[0, 4:12] = own[2]
    pr[0, 12:15] = above(nxt[7:10])
    for d, f, at, vy, after in ((ds, 0, 4, 7, 4), (dr, 1, 11, 14, 10)):
        d[1:4] = below(prev[at : at + 3])
        d[4] = own[2 * f + 1, 0] - below(prev[vy])
        d[5:12] = own[2 * f + 1, 1:8]
        d[12] = above(nxt[after] - mine[vy])
        d[13:15] = above(nxt[after + 1 : after + 3])
    run, first = stepper(ps, pr, ds, dr, mod, buoy, add_s, add_r)
    first(4, 12)
    run(0, [(5, (0,)), (8, (0,))], 3)
    run(0, [(11, (0,))], 1, 1)
    run(1, [(6, (0, 1)), (8, (0, 1))], 2)
    run(1, [(5, (1,)), (10, (0, 1))], 1, 1)
    run(2, [(7, (0, 1)), (8, (0, 1))], 1, 1)
    run(2, [(6, (1,)), (9, (0, 1))], 1, 1)
    run(3, [(7, (1,)), (8, (0, 1))], 1, 1)


def outer_kernel(
    anchors, model_prev, model_next, add_s, add_r, ps_in, pr_in, ds_in, dr_in, mod_in, buoy_in,
    keep, send, ps, pr, ds, dr, mod, buoy, corr,
):
    del ps_in, pr_in, ds_in, dr_in, mod_in, buoy_in
    below, above = inner_tile()
    mod[1:4] = below(model_prev[0:3])
    mod[12:15] = above(model_next[0:3])
    buoy[0:4] = below(model_prev[3:7])
    buoy[12:15] = above(model_next[3:6])
    keep[...] = jnp.zeros(keep.shape, F32)
    send[...] = jnp.zeros(send.shape, F32)
    run, first = stepper(ps, pr, ds, dr, mod, buoy, add_s, add_r)
    first(1, 4)
    first(12, 15)
    for s in range(STEPS):
        both = (0, 1) if s else (0,)
        run(s, [(s + 1, both), (12 - s, both), (s + 4, (0,))], 1, 1)
        run(s, [(s + 2, both), (13 - s, both)], 2, INLINE)

    def image(y, _):
        value = ps[4, y] * (pr[1, y] + add_r[3, y]) + ps[3, y] * (pr[2, y] + add_r[2, y])
        value += ps[2, y] * (pr[3, y] + add_r[1, y]) + ps[1, y] * (pr[4, y] + add_r[0, y])
        corr[pl.ds(y - STEPS, ROWS, stride=COLS), :] = value / STEPS
        return 0

    lax.fori_loop(STEPS, STEPS + COLS, image, 0, unroll=2)

    c, g = place()
    odd = (c + anchors[g]) & 1
    for out, start in ((keep, odd), (send, 1 - odd)):
        at = (anchors[g] + start) >> 1
        for i in range(8):
            out[at + i] = corr[pl.ds(pl.multiple_of(32 * (start + 2 * i), 32), 32), :]


STATE = [shape(STEPS + 1, PLANES, ROWS, DEPTH)] * 2 + [shape(PLANES, ROWS, DEPTH)] * 4


def inner(*operands):
    return pl.pallas_call(
        inner_kernel,
        out_shape=STATE,
        in_specs=[VMEM] * 7,
        out_specs=[VMEM] * 6,
        compiler_params=params(4),
        cost_estimate=COST,
        name="inner",
    )(*operands)


def outer(*operands):
    return pl.pallas_call(
        outer_kernel,
        out_shape=[shape(16, 32, DEPTH)] * 2 + STATE,
        in_specs=[SMEM] + [VMEM] * 10,
        out_specs=[VMEM] * 8,
        scratch_shapes=[pltpu.VMEM((COLS * ROWS, DEPTH), F32)],
        input_output_aliases={5 + i: 2 + i for i in range(6)},
        compiler_params=params(4),
        name="outer",
    )(*operands)[:2]


def halve_kernel(keep, got, s0, s1, s2, s3):
    x = lax.axis_index("x")
    for d, out in enumerate((s0, s1, s2, s3)):
        at = ((x + d) & (NX - 1)) * NZH
        for i in range(NZH):
            out[i] = keep[at + i] + got[at + i]


def quarter_kernel(s0, r1, r2, r3, u0, u1, u2, u3):
    z = lax.axis_index("zh")
    for d, out in enumerate((u0, u1, u2, u3)):
        at = (z + d) & (NZH - 1)
        out[...] = (s0[at] + r1[at]) + (r2[at] + r3[at])


def last_kernel(u0, q1, q2, q3, out):
    out[...] = (u0[...] + q1[...]) + (q2[...] + q3[...])


def other_core(block):
    return lax.ppermute(block, "core", [(0, 1), (1, 0)])


def to_tile(block, distance):
    return lax.ppermute(block, "tile", [(i, (i + distance) % NT) for i in range(NT)])


def along(blocks, axis, order):
    return [lax.ppermute(blocks[d - 1], axis, [(i, (i + d) % 4) for i in range(4)]) for d in order]


def local(velocity, density, anchors, src_state, rcv_state, src_pos, wavelet, rec_pos, traces):
    plane = (ROWS, DEPTH)
    strip = jnp.stack([velocity, density])[None]
    zs = along([strip] * 3, "zh", GATHER)

    own, to_prev, to_next, anchors = pl.pallas_call(
        pack_kernel,
        out_shape=[
            shape(4, COLS * ROWS, DEPTH),
            shape(13, *plane),
            shape(15, *plane),
            jax.ShapeDtypeStruct(anchors.shape, anchors.dtype),
        ],
        in_specs=[HBM] * 3,
        out_specs=[VMEM] * 4,
        scratch_shapes=[
            pltpu.VMEM((4, ROWS, COLS, DEPTH), F32),
            pltpu.VMEM((4, ROWS, COLS, DEPTH), F32),
            pltpu.SemaphoreType.DMA((2, 2)),
            pltpu.SemaphoreType.DMA,
        ],
        compiler_params=params(8),
        name="pack",
    )(*(pltpu.with_memory_space_constraint(a, pltpu.HBM) for a in (src_state, rcv_state, anchors)))
    *zs, own, to_prev, to_next = lax.optimization_barrier((*zs, own, to_prev, to_next))

    xs = [jnp.concatenate([strip, *zs])]
    xs += along([xs[0]] * 3, "x", GATHER)

    halo_next = to_tile(to_prev, -1)
    halo_prev = to_tile(to_next, 1)

    inj_src, inj_rec = pl.pallas_call(
        inject_kernel,
        out_shape=[shape(STEPS, PLANES, *plane)] * 2,
        in_specs=[SMEM] * 4,
        out_specs=[VMEM] * 2,
        compiler_params=params(2),
        name="inject",
    )(src_pos, wavelet[0].T, rec_pos, traces[0].T)

    *mine, other_m, other_b = pl.pallas_call(
        window_kernel,
        out_shape=[shape(8, *strip.shape[2:])] * 4,
        in_specs=[SMEM] + [VMEM] * 4,
        out_specs=[VMEM] * 4,
        compiler_params=params(2),
        name="window",
    )(anchors, *xs)
    got = [other_core(o) for o in (other_m, other_b)]

    mb, mb_prev, mb_next = pl.pallas_call(
        model_kernel,
        out_shape=[shape(2, COLS * ROWS, DEPTH), shape(6, *plane), shape(7, *plane)],
        in_specs=[SMEM] + [VMEM] * 4,
        out_specs=[VMEM] * 3,
        compiler_params=params(2),
        name="model",
    )(anchors, *mine, *got)
    model_next = to_tile(mb_prev, -1)
    model_prev = to_tile(mb_next, 1)

    state = inner(
        own.reshape(4, COLS, *plane),
        halo_prev,
        halo_next,
        to_next,
        mb.reshape(2, COLS, *plane),
        inj_src,
        inj_rec,
    )
    keep, send = outer(anchors, model_prev, model_next, inj_src, inj_rec, *state)

    parts = pl.pallas_call(
        halve_kernel,
        out_shape=[shape(NZH, 32, DEPTH)] * NX,
        in_specs=[VMEM, VMEM],
        out_specs=[VMEM] * NX,
        compiler_params=params(2),
        name="halve",
    )(keep, other_core(send))
    moved = along(parts[1:], "x", SCATTER)
    parts = pl.pallas_call(
        quarter_kernel,
        out_shape=[shape(32, DEPTH)] * NZH,
        in_specs=[VMEM] * NX,
        out_specs=[VMEM] * NZH,
        compiler_params=params(2),
        name="quarter",
    )(parts[0], *moved)
    moved = along(parts[1:], "zh", SCATTER)
    image = pl.pallas_call(
        last_kernel,
        out_shape=shape(32, DEPTH),
        in_specs=[VMEM] * NZH,
        out_specs=VMEM,
        compiler_params=params(2),
        name="last",
    )(parts[0], *moved)
    return image.reshape(velocity.shape)


def solution(mesh):
    shot = ("x", "zh", "core")
    return jax.shard_map(
        local,
        mesh=Mesh(mesh.devices.reshape(NX, NZH, NC, NT), (*shot, "tile")),
        in_specs=(
            P(shot, "tile", None),
            P(shot, "tile", None),
            P(),
            P(None, shot, "tile", None),
            P(None, shot, "tile", None),
            P(shot, None),
            P(shot, None, None),
            P(shot, None),
            P(shot, None, None),
        ),
        out_specs=P(shot, "tile", None),
        check_vma=False,
    )
```

```python
import functools

import jax
import jax.numpy as jnp
from jax import lax
from jax.experimental import pallas as pl
from jax.experimental.pallas import tpu as pltpu
from jax.sharding import Mesh
from jax.sharding import PartitionSpec as P

STEPS = 4
INLINE = 1
COST = None
GATHER, SCATTER = (3, 1, 2), (2, 1, 3)
F32 = jnp.float32
ROWS = 64
COLS = 8
DEPTH = 128
PLANES = COLS + 2 * STEPS
NX, NZH, NC, NT = 4, 4, 2, 8

VMEM = pl.BlockSpec(memory_space=pltpu.VMEM)
SMEM = pl.BlockSpec(memory_space=pltpu.SMEM)
ANY = pl.BlockSpec(memory_space=pl.ANY)
HBM = pl.BlockSpec(memory_space=pltpu.HBM)


def shape(*dims):
    return jax.ShapeDtypeStruct(dims, F32)


def params(mib):
    return pltpu.CompilerParams(vmem_limit_bytes=mib * 1024 * 1024)


def place():
    c = lax.axis_index("core")
    return c, (lax.axis_index("x") * NZH + lax.axis_index("zh")) * NC + c


def anchor(anchors, g):
    lane = lax.broadcasted_iota(jnp.int32, anchors.shape, 1)
    return jnp.sum(jnp.where(lane == g, anchors[...], 0))


def first_strip(b, c):
    return (b + ((c + b) & 1)) >> 1


def pack_kernel(src_in, rcv_in, anchors_in, own, to_prev, to_next, anchors, src, rcv, sem, anchors_sem):
    held = pltpu.make_async_copy(anchors_in, anchors, anchors_sem)
    held.start()
    half = ROWS // 2
    copies = []
    for h in range(2):
        cut = slice(h * half, h * half + half)
        for f, (a, b) in enumerate(((src_in, src), (rcv_in, rcv))):
            copies.append(pltpu.make_async_copy(a.at[:, cut], b.at[:, cut], sem.at[h, f]))
            copies[-1].start()
    lane = lax.broadcasted_iota(jnp.int32, (COLS, DEPTH), 1)
    col = lax.broadcasted_iota(jnp.int32, (COLS, DEPTH), 0)

    def row(x, before):
        after = []
        for f, state in enumerate((src, rcv)):
            p, vx, vy, vz = (state[i, x] for i in range(4))
            spread = vx - before[f]
            spread += vy - jnp.where(col == 0, 0.0, pltpu.roll(vy, 1, 0))
            spread += vz - jnp.where(lane == 0, 0.0, pltpu.roll(vz, 1, 1))
            own[2 * f, pl.ds(x, COLS, stride=ROWS), :] = p
            own[2 * f + 1, pl.ds(x, COLS, stride=ROWS), :] = spread
            to_next[7 + 7 * f, pl.ds(x, 1), :] = vy[COLS - 1 :, :]
            after.append(vx)
        return tuple(after)

    before = (jnp.zeros((COLS, DEPTH), F32),) * 2
    for h in range(2):
        for copy in copies[2 * h : 2 * h + 2]:
            copy.wait()
        before = lax.fori_loop(h * half, h * half + half, row, before, unroll=8)

    held.wait()

    def plane(f, y):
        return own[f, y * ROWS : (y + 1) * ROWS, :]

    for i, (f, y) in enumerate(
        [(0, 0), (0, 1), (0, 2), (0, 3), (1, 0), (1, 1), (1, 2)]
        + [(2, 0), (2, 1), (2, 2), (3, 0), (3, 1), (3, 2)]
    ):
        to_prev[i] = plane(f, y)
    for i, (f, y) in (
        list(enumerate([(0, 4), (0, 5), (0, 6), (0, 7), (1, 5), (1, 6), (1, 7)]))
        + list(enumerate([(2, 5), (2, 6), (2, 7), (3, 5), (3, 6), (3, 7)], 8))
    ):
        to_next[i] = plane(f, y)


def inject_kernel(src_pos, wavelet, rec_pos, traces, src_out, rec_out):
    for out in (src_out, rec_out):
        for s in range(STEPS):
            out[s, 1 : PLANES - 1] = jnp.zeros((PLANES - 2, ROWS, DEPTH), F32)
    first = lax.axis_index("tile") * COLS - STEPS
    lane = lax.broadcasted_iota(jnp.int32, (1, DEPTH), 1)
    for pos, amp, out in ((src_pos, wavelet, src_out), (rec_pos, traces, rec_out)):

        def point(k, _, pos=pos, amp=amp, out=out):
            cell = pos[0, k]
            x = cell >> 13
            y = jnp.clip(((cell >> 7) & (COLS * NT - 1)) - first, 0, PLANES - 1)
            hit = lane == (cell & (DEPTH - 1))
            old = [out[s, y, pl.ds(x, 1), :] for s in range(STEPS)]
            for s in range(STEPS):
                out[s, y, pl.ds(x, 1), :] = old[s] + jnp.where(hit, amp[s, k], 0.0)
            return 0

        lax.fori_loop(0, pos.shape[1], point, 0, unroll=8)


def window_kernel(offset, anchors, a0, a1, a2, a3, modulus, buoyancy):
    x, z = lax.axis_index("x"), lax.axis_index("zh")
    c, g = place()
    first = first_strip(anchor(anchors, g + offset * (1 - 2 * c)), c)
    for dx, strips in zip((0, *GATHER), (a0, a1, a2, a3)):
        for dz, at in zip((0, *GATHER), range(NZH)):
            i = ((x - dx) & (NX - 1)) * NZH + ((z - dz) & (NZH - 1)) - first

            @pl.when((i >= 0) & (i < 8))
            def _(i=i, strips=strips, at=at):
                vel, den = strips[at, 0], strips[at, 1]
                modulus[i] = den * vel * vel
                buoyancy[i] = 1.0 / den


def strip_rows(anchors, own_m, own_b, other_m, other_b):
    c, g = place()
    odd = (c + anchor(anchors, g)) & 1
    for m, b, start in ((own_m, own_b, odd), (other_m, other_b, 1 - odd)):
        for i in range(8):
            for r in range(4):
                yield 4 * (start + 2 * i) + r, m[i, r], b[i, r]


def edge_kernel(anchors, own_m, own_b, other_m, other_b, to_prev, to_next):
    for x, m, b in strip_rows(anchors, own_m, own_b, other_m, other_b):
        to_prev[pl.ds(x, 3, stride=ROWS), :] = m[:3]
        to_prev[pl.ds(x + 3 * ROWS, 3, stride=ROWS), :] = b[:3]
        to_next[pl.ds(x, 3, stride=ROWS), :] = m[5:]
        to_next[pl.ds(x + 3 * ROWS, 4, stride=ROWS), :] = b[4:]


def model_kernel(anchors, own_m, own_b, other_m, other_b, out):
    for x, m, b in strip_rows(anchors, own_m, own_b, other_m, other_b):
        out[0, pl.ds(x, COLS, stride=ROWS), :] = m
        out[1, pl.ds(x, COLS, stride=ROWS), :] = b


def inner_tile():
    tile = lax.axis_index("tile")
    low, high = tile > 0, tile < NT - 1
    return (lambda value: jnp.where(low, value, 0.0)), (lambda value: jnp.where(high, value, 0.0))


def stepper(ps, pr, ds, dr, mod, buoy, add_s, add_r):
    lane = lax.broadcasted_iota(jnp.int32, (8, DEPTH), 1)
    row = lax.broadcasted_iota(jnp.int32, (8, DEPTH), 0)
    first_lane, last_lane, first_row, last_row = lane == 0, lane == DEPTH - 1, row == 0, row == 7
    blocks = range(ROWS // 8)
    zero = jnp.zeros((8, DEPTH), F32)
    fields = ((ps, ds, add_s, lambda s: s), (pr, dr, add_r, lambda s: STEPS - s))

    def get(ref, *at):
        return [ref[(*at, slice(8 * v, 8 * v + 8))] for v in blocks]

    def spread_of(p, after, before, b):
        down = [pltpu.roll(p[v], 7, 0) for v in blocks] + [zero]
        flux_y = [b[v] * (after[v] - p[v]) for v in blocks]
        out, last = [], zero
        for v in blocks:
            flux_x = b[v] * (jnp.where(last_row, down[v + 1], down[v]) - p[v])
            flux_z = b[v] * (jnp.where(last_lane, 0.0, pltpu.roll(p[v], DEPTH - 1, 1)) - p[v])
            turned = pltpu.roll(flux_x, 1, 0)
            spread = (flux_x - jnp.where(first_row, last, turned)) + (flux_y[v] - before[v])
            spread += flux_z - jnp.where(first_lane, 0.0, pltpu.roll(flux_z, 1, 1))
            last = turned
            out.append(spread)
        return out, flux_y

    def plane(s, y, wanted, carry):
        m, b = get(mod, y), get(buoy, y)
        ends = []
        for f, (p, before) in zip(wanted, carry):
            p_all, d_all, add, amp = fields[f]
            after = get(p_all, s, y + 1)
            spread, flux = spread_of(p, after, before, b)
            ends.append((after, flux))
            for v in blocks:
                cut = slice(8 * v, 8 * v + 8)
                d = d_all[y, cut] - spread[v]
                p_all[s + 1, y, cut] = p[v] + add[amp(s), y, cut] - m[v] * d
                if s < STEPS - 1:
                    d_all[y, cut] = d
        return ends

    def run(s, groups, count, inline=0):
        carry = []
        for y, wanted in groups:
            b, part = get(buoy, y - 1), []
            for f in wanted:
                here, before = get(fields[f][0], s, y), get(fields[f][0], s, y - 1)
                part.append((here, [b[v] * (here[v] - before[v]) for v in blocks]))
            carry.append(part)

        def planes(i, carry):
            return [plane(s, y + i, wanted, part) for (y, wanted), part in zip(groups, carry)]

        if inline:
            for i in range(count):
                carry = planes(i, carry)
        else:
            lax.fori_loop(0, count, planes, carry)

    def first(low, high):
        for y in range(low, high):
            for v in blocks:
                cut = slice(8 * v, 8 * v + 8)
                pr[1, y, cut] = pr[0, y, cut] - mod[y, cut] * dr[y, cut]

    return run, first


def inner_kernel(own, prev, nxt, mine, model, add_s, add_r, ps, pr, ds, dr, mod, buoy):
    below, above = inner_tile()
    mod[4:12] = model[0]
    buoy[4:12] = model[1]
    ps[0, 0:4] = below(prev[0:4])
    ps[0, 4:12] = own[0]
    ps[0, 12:16] = above(nxt[0:4])
    pr[0, 1:4] = below(prev[8:11])
    pr[0, 4:12] = own[2]
    pr[0, 12:15] = above(nxt[7:10])
    for d, f, at, vy, after in ((ds, 0, 4, 7, 4), (dr, 1, 11, 14, 10)):
        d[1:4] = below(prev[at : at + 3])
        d[4] = own[2 * f + 1, 0] - below(prev[vy])
        d[5:12] = own[2 * f + 1, 1:8]
        d[12] = above(nxt[after] - mine[vy])
        d[13:15] = above(nxt[after + 1 : after + 3])
    run, first = stepper(ps, pr, ds, dr, mod, buoy, add_s, add_r)
    first(4, 12)
    run(0, [(5, (0,)), (8, (0,))], 3)
    run(0, [(11, (0,))], 1, 1)
    run(1, [(6, (0, 1)), (8, (0, 1))], 2)
    run(1, [(5, (1,)), (10, (0, 1))], 1, 1)
    run(2, [(7, (0, 1)), (8, (0, 1))], 1, 1)
    run(2, [(6, (1,)), (9, (0, 1))], 1, 1)
    run(3, [(7, (1,)), (8, (0, 1))], 1, 1)


def outer_kernel(
    anchors, model_prev, model_next, add_s, add_r, ps_in, pr_in, ds_in, dr_in, mod_in, buoy_in,
    keep, send, ps, pr, ds, dr, mod, buoy, corr,
):
    del ps_in, pr_in, ds_in, dr_in, mod_in, buoy_in
    below, above = inner_tile()
    mod[1:4] = below(model_prev[0:3])
    mod[12:15] = above(model_next[0:3])
    buoy[0:4] = below(model_prev[3:7])
    buoy[12:15] = above(model_next[3:6])
    keep[...] = jnp.zeros(keep.shape, F32)
    send[...] = jnp.zeros(send.shape, F32)
    run, first = stepper(ps, pr, ds, dr, mod, buoy, add_s, add_r)
    first(1, 4)
    first(12, 15)
    for s in range(STEPS):
        both = (0, 1) if s else (0,)
        run(s, [(s + 1, both), (12 - s, both), (s + 4, (0,))], 1, 1)
        run(s, [(s + 2, both), (13 - s, both)], 2, INLINE)

    def image(y, _):
        value = ps[4, y] * (pr[1, y] + add_r[3, y]) + ps[3, y] * (pr[2, y] + add_r[2, y])
        value += ps[2, y] * (pr[3, y] + add_r[1, y]) + ps[1, y] * (pr[4, y] + add_r[0, y])
        corr[pl.ds(y - STEPS, ROWS, stride=COLS), :] = value / STEPS
        return 0

    lax.fori_loop(STEPS, STEPS + COLS, image, 0, unroll=2)

    c, g = place()
    b = anchor(anchors, g)
    odd = (c + b) & 1
    for out, start in ((keep, odd), (send, 1 - odd)):
        at = (b + start) >> 1
        for i in range(8):
            out[at + i] = corr[pl.ds(pl.multiple_of(32 * (start + 2 * i), 32), 32), :]


STATE = [shape(STEPS + 1, PLANES, ROWS, DEPTH)] * 2 + [shape(PLANES, ROWS, DEPTH)] * 4


def inner(*operands):
    return pl.pallas_call(
        inner_kernel,
        out_shape=STATE,
        in_specs=[VMEM] * 7,
        out_specs=[VMEM] * 6,
        compiler_params=params(4),
        cost_estimate=COST,
        name="inner",
    )(*operands)


def outer(*operands):
    return pl.pallas_call(
        outer_kernel,
        out_shape=[shape(16, 32, DEPTH)] * 2 + STATE,
        in_specs=[VMEM] * 11,
        out_specs=[VMEM] * 8,
        scratch_shapes=[pltpu.VMEM((COLS * ROWS, DEPTH), F32)],
        input_output_aliases={5 + i: 2 + i for i in range(6)},
        compiler_params=params(4),
        name="outer",
    )(*operands)[:2]


def halve_kernel(keep, got, s0, s1, s2, s3):
    x = lax.axis_index("x")
    for d, out in enumerate((s0, s1, s2, s3)):
        at = ((x + d) & (NX - 1)) * NZH
        for i in range(NZH):
            out[i] = keep[at + i] + got[at + i]


def quarter_kernel(s0, r1, r2, r3, u0, u1, u2, u3):
    z = lax.axis_index("zh")
    for d, out in enumerate((u0, u1, u2, u3)):
        at = (z + d) & (NZH - 1)
        out[...] = (s0[at] + r1[at]) + (r2[at] + r3[at])


def last_kernel(u0, q1, q2, q3, out):
    out[...] = (u0[...] + q1[...]) + (q2[...] + q3[...])


def other_core(block):
    return lax.ppermute(block, "core", [(0, 1), (1, 0)])


def to_tile(block, distance):
    return lax.ppermute(block, "tile", [(i, (i + distance) % NT) for i in range(NT)])


def along(blocks, axis, order):
    return [lax.ppermute(blocks[d - 1], axis, [(i, (i + d) % 4) for i in range(4)]) for d in order]


def local(velocity, density, anchors, src_state, rcv_state, src_pos, wavelet, rec_pos, traces):
    plane = (ROWS, DEPTH)
    strip = jnp.stack([velocity, density])[None]
    zs = along([strip] * 3, "zh", GATHER)

    own, to_prev, to_next, anchors = pl.pallas_call(
        pack_kernel,
        out_shape=[
            shape(4, COLS * ROWS, DEPTH),
            shape(13, *plane),
            shape(15, *plane),
            jax.ShapeDtypeStruct((1, *anchors.shape), anchors.dtype),
        ],
        in_specs=[HBM] * 3,
        out_specs=[VMEM] * 4,
        scratch_shapes=[
            pltpu.VMEM((4, ROWS, COLS, DEPTH), F32),
            pltpu.VMEM((4, ROWS, COLS, DEPTH), F32),
            pltpu.SemaphoreType.DMA((2, 2)),
            pltpu.SemaphoreType.DMA,
        ],
        compiler_params=params(8),
        name="pack",
    )(*(pltpu.with_memory_space_constraint(a, pltpu.HBM) for a in (src_state, rcv_state, anchors[None])))
    *zs, own, to_prev, to_next = lax.optimization_barrier((*zs, own, to_prev, to_next))

    xs = [jnp.concatenate([strip, *zs])]
    xs += along([xs[0]] * 3, "x", GATHER)

    halo_next = to_tile(to_prev, -1)
    halo_prev = to_tile(to_next, 1)

    inj_src, inj_rec = pl.pallas_call(
        inject_kernel,
        out_shape=[shape(STEPS, PLANES, *plane)] * 2,
        in_specs=[SMEM] * 4,
        out_specs=[VMEM] * 2,
        compiler_params=params(2),
        name="inject",
    )(src_pos, wavelet[0].T, rec_pos, traces[0].T)

    other, mine = [
        pl.pallas_call(
            functools.partial(window_kernel, offset),
            out_shape=[shape(8, *strip.shape[2:])] * 2,
            in_specs=[VMEM] * 5,
            out_specs=[VMEM] * 2,
            compiler_params=params(2),
            name="window%d" % offset,
        )(anchors, *xs)
        for offset in (1, 0)
    ]
    model = (anchors, *mine, *(other_core(block) for block in other))
    edge_prev, edge_next = pl.pallas_call(
        edge_kernel,
        out_shape=[shape(6 * ROWS, DEPTH), shape(7 * ROWS, DEPTH)],
        in_specs=[VMEM] * 5,
        out_specs=[VMEM] * 2,
        compiler_params=params(2),
        name="edge",
    )(*model)
    model_next = to_tile(edge_prev.reshape(6, *plane), -1)
    model_prev = to_tile(edge_next.reshape(7, *plane), 1)
    mb = pl.pallas_call(
        model_kernel,
        out_shape=shape(2, COLS * ROWS, DEPTH),
        in_specs=[VMEM] * 5,
        out_specs=VMEM,
        compiler_params=params(2),
        name="model",
    )(*model)

    state = inner(
        own.reshape(4, COLS, *plane),
        halo_prev,
        halo_next,
        to_next,
        mb.reshape(2, COLS, *plane),
        inj_src,
        inj_rec,
    )
    keep, send = outer(anchors, model_prev, model_next, inj_src, inj_rec, *state)

    parts = pl.pallas_call(
        halve_kernel,
        out_shape=[shape(NZH, 32, DEPTH)] * NX,
        in_specs=[VMEM, VMEM],
        out_specs=[VMEM] * NX,
        compiler_params=params(2),
        name="halve",
    )(keep, other_core(send))
    moved = along(parts[1:], "x", SCATTER)
    parts = pl.pallas_call(
        quarter_kernel,
        out_shape=[shape(32, DEPTH)] * NZH,
        in_specs=[VMEM] * NX,
        out_specs=[VMEM] * NZH,
        compiler_params=params(2),
        name="quarter",
    )(parts[0], *moved)
    moved = along(parts[1:], "zh", SCATTER)
    image = pl.pallas_call(
        last_kernel,
        out_shape=shape(32, DEPTH),
        in_specs=[VMEM] * NZH,
        out_specs=VMEM,
        compiler_params=params(2),
        name="last",
    )(parts[0], *moved)
    return image.reshape(velocity.shape)


def solution(mesh):
    shot = ("x", "zh", "core")
    return jax.shard_map(
        local,
        mesh=Mesh(mesh.devices.reshape(NX, NZH, NC, NT), (*shot, "tile")),
        in_specs=(
            P(shot, "tile", None),
            P(shot, "tile", None),
            P(),
            P(None, shot, "tile", None),
            P(None, shot, "tile", None),
            P(shot, None),
            P(shot, None, None),
            P(shot, None),
            P(shot, None, None),
        ),
        out_specs=P(shot, "tile", None),
        check_vma=False,
    )
```

```python
import functools

import jax
import jax.numpy as jnp
from jax import lax
from jax.experimental import pallas as pl
from jax.experimental.pallas import tpu as pltpu
from jax.sharding import Mesh
from jax.sharding import PartitionSpec as P

STEPS = 4
INLINE = 1
COST = None
GATHER, SCATTER = (3, 1, 2), (2, 1, 3)
F32 = jnp.float32
ROWS = 64
COLS = 8
DEPTH = 128
PLANES = COLS + 2 * STEPS
NX, NZH, NC, NT = 4, 4, 2, 8

VMEM = pl.BlockSpec(memory_space=pltpu.VMEM)
SMEM = pl.BlockSpec(memory_space=pltpu.SMEM)
ANY = pl.BlockSpec(memory_space=pl.ANY)
HBM = pl.BlockSpec(memory_space=pltpu.HBM)


def shape(*dims):
    return jax.ShapeDtypeStruct(dims, F32)


def params(mib):
    return pltpu.CompilerParams(vmem_limit_bytes=mib * 1024 * 1024)


def place():
    c = lax.axis_index("core")
    return c, (lax.axis_index("x") * NZH + lax.axis_index("zh")) * NC + c


def anchor(anchors, g):
    lane = lax.broadcasted_iota(jnp.int32, anchors.shape, 1)
    return jnp.sum(jnp.where(lane == g, anchors[...], 0))


def first_strip(b, c):
    return (b + ((c + b) & 1)) >> 1


def pack_kernel(src_in, rcv_in, anchors_in, own, to_prev, to_next, anchors, src, rcv, sem, anchors_sem):
    held = pltpu.make_async_copy(anchors_in, anchors, anchors_sem)
    held.start()
    half = ROWS // 2
    copies = []
    for h in range(2):
        cut = slice(h * half, h * half + half)
        for f, (a, b) in enumerate(((src_in, src), (rcv_in, rcv))):
            copies.append(pltpu.make_async_copy(a.at[:, cut], b.at[:, cut], sem.at[h, f]))
            copies[-1].start()
    lane = lax.broadcasted_iota(jnp.int32, (COLS, DEPTH), 1)
    col = lax.broadcasted_iota(jnp.int32, (COLS, DEPTH), 0)

    def row(x, before):
        after = []
        for f, state in enumerate((src, rcv)):
            p, vx, vy, vz = (state[i, x] for i in range(4))
            spread = vx - before[f]
            spread += vy - jnp.where(col == 0, 0.0, pltpu.roll(vy, 1, 0))
            spread += vz - jnp.where(lane == 0, 0.0, pltpu.roll(vz, 1, 1))
            own[2 * f, pl.ds(x, COLS, stride=ROWS), :] = p
            own[2 * f + 1, pl.ds(x, COLS, stride=ROWS), :] = spread
            to_next[7 + 7 * f, pl.ds(x, 1), :] = vy[COLS - 1 :, :]
            after.append(vx)
        return tuple(after)

    before = (jnp.zeros((COLS, DEPTH), F32),) * 2
    for h in range(2):
        for copy in copies[2 * h : 2 * h + 2]:
            copy.wait()
        before = lax.fori_loop(h * half, h * half + half, row, before, unroll=8)

    held.wait()

    def plane(f, y):
        return own[f, y * ROWS : (y + 1) * ROWS, :]

    for i, (f, y) in enumerate(
        [(0, 0), (0, 1), (0, 2), (0, 3), (1, 0), (1, 1), (1, 2)]
        + [(2, 0), (2, 1), (2, 2), (3, 0), (3, 1), (3, 2)]
    ):
        to_prev[i] = plane(f, y)
    for i, (f, y) in (
        list(enumerate([(0, 4), (0, 5), (0, 6), (0, 7), (1, 5), (1, 6), (1, 7)]))
        + list(enumerate([(2, 5), (2, 6), (2, 7), (3, 5), (3, 6), (3, 7)], 8))
    ):
        to_next[i] = plane(f, y)


def inject_kernel(src_pos, wavelet, rec_pos, traces, src_out, rec_out):
    for out in (src_out, rec_out):
        for s in range(STEPS):
            out[s, 1 : PLANES - 1] = jnp.zeros((PLANES - 2, ROWS, DEPTH), F32)
    first = lax.axis_index("tile") * COLS - STEPS
    lane = lax.broadcasted_iota(jnp.int32, (1, DEPTH), 1)
    for pos, amp, out in ((src_pos, wavelet, src_out), (rec_pos, traces, rec_out)):

        def point(k, _, pos=pos, amp=amp, out=out):
            cell = pos[0, k]
            x = cell >> 13
            y = jnp.clip(((cell >> 7) & (COLS * NT - 1)) - first, 0, PLANES - 1)
            hit = lane == (cell & (DEPTH - 1))
            old = [out[s, y, pl.ds(x, 1), :] for s in range(STEPS)]
            for s in range(STEPS):
                out[s, y, pl.ds(x, 1), :] = old[s] + jnp.where(hit, amp[s, k], 0.0)
            return 0

        lax.fori_loop(0, pos.shape[1], point, 0, unroll=8)


def window_kernel(offset, anchors, a0, a1, a2, a3, modulus, buoyancy):
    x, z = lax.axis_index("x"), lax.axis_index("zh")
    c, g = place()
    first = first_strip(anchor(anchors, g + offset * (1 - 2 * c)), c)
    for dx, strips in zip((0, *GATHER), (a0, a1, a2, a3)):
        for dz, at in zip((0, *GATHER), range(NZH)):
            i = ((x - dx) & (NX - 1)) * NZH + ((z - dz) & (NZH - 1)) - first

            @pl.when((i >= 0) & (i < 8))
            def _(i=i, strips=strips, at=at):
                vel, den = strips[at, 0], strips[at, 1]
                modulus[i] = den * vel * vel
                buoyancy[i] = 1.0 / den


def strip_rows(anchors, own_m, own_b, other_m, other_b):
    c, g = place()
    odd = (c + anchor(anchors, g)) & 1
    for m, b, start in ((own_m, own_b, odd), (other_m, other_b, 1 - odd)):
        for i in range(8):
            for r in range(4):
                yield 4 * (start + 2 * i) + r, m[i, r], b[i, r]


def edge_kernel(anchors, own_m, own_b, other_m, other_b, to_prev, to_next):
    for x, m, b in strip_rows(anchors, own_m, own_b, other_m, other_b):
        to_prev[pl.ds(x, 3, stride=ROWS), :] = m[:3]
        to_prev[pl.ds(x + 3 * ROWS, 3, stride=ROWS), :] = b[:3]
        to_next[pl.ds(x, 3, stride=ROWS), :] = m[5:]
        to_next[pl.ds(x + 3 * ROWS, 4, stride=ROWS), :] = b[4:]


def model_kernel(anchors, own_m, own_b, other_m, other_b, out):
    for x, m, b in strip_rows(anchors, own_m, own_b, other_m, other_b):
        out[0, pl.ds(x, COLS, stride=ROWS), :] = m
        out[1, pl.ds(x, COLS, stride=ROWS), :] = b


def inner_tile():
    tile = lax.axis_index("tile")
    low, high = tile > 0, tile < NT - 1
    return (lambda value: jnp.where(low, value, 0.0)), (lambda value: jnp.where(high, value, 0.0))


def stepper(ps, pr, ds, dr, mod, buoy, add_s, add_r):
    lane = lax.broadcasted_iota(jnp.int32, (8, DEPTH), 1)
    row = lax.broadcasted_iota(jnp.int32, (8, DEPTH), 0)
    first_lane, last_lane, first_row, last_row = lane == 0, lane == DEPTH - 1, row == 0, row == 7
    blocks = range(ROWS // 8)
    zero = jnp.zeros((8, DEPTH), F32)
    fields = ((ps, ds, add_s, lambda s: s), (pr, dr, add_r, lambda s: STEPS - s))

    def get(ref, *at):
        return [ref[(*at, slice(8 * v, 8 * v + 8))] for v in blocks]

    def spread_of(p, after, before, b):
        down = [pltpu.roll(p[v], 7, 0) for v in blocks] + [zero]
        flux_y = [b[v] * (after[v] - p[v]) for v in blocks]
        out, last = [], zero
        for v in blocks:
            flux_x = b[v] * (jnp.where(last_row, down[v + 1], down[v]) - p[v])
            flux_z = b[v] * (jnp.where(last_lane, 0.0, pltpu.roll(p[v], DEPTH - 1, 1)) - p[v])
            turned = pltpu.roll(flux_x, 1, 0)
            spread = (flux_x - jnp.where(first_row, last, turned)) + (flux_y[v] - before[v])
            spread += flux_z - jnp.where(first_lane, 0.0, pltpu.roll(flux_z, 1, 1))
            last = turned
            out.append(spread)
        return out, flux_y

    def plane(s, y, wanted, carry):
        m, b = get(mod, y), get(buoy, y)
        ends = []
        for f, (p, before) in zip(wanted, carry):
            p_all, d_all, add, amp = fields[f]
            after = get(p_all, s, y + 1)
            spread, flux = spread_of(p, after, before, b)
            ends.append((after, flux))
            for v in blocks:
                cut = slice(8 * v, 8 * v + 8)
                d = d_all[y, cut] - spread[v]
                p_all[s + 1, y, cut] = p[v] + add[amp(s), y, cut] - m[v] * d
                if s < STEPS - 1:
                    d_all[y, cut] = d
        return ends

    def run(s, groups, count, inline=0):
        carry = []
        for y, wanted in groups:
            b, part = get(buoy, y - 1), []
            for f in wanted:
                here, before = get(fields[f][0], s, y), get(fields[f][0], s, y - 1)
                part.append((here, [b[v] * (here[v] - before[v]) for v in blocks]))
            carry.append(part)

        def planes(i, carry):
            return [plane(s, y + i, wanted, part) for (y, wanted), part in zip(groups, carry)]

        if inline:
            for i in range(count):
                carry = planes(i, carry)
        else:
            lax.fori_loop(0, count, planes, carry)

    def first(low, high):
        for y in range(low, high):
            for v in blocks:
                cut = slice(8 * v, 8 * v + 8)
                pr[1, y, cut] = pr[0, y, cut] - mod[y, cut] * dr[y, cut]

    return run, first


def inner_kernel(own, prev, nxt, mine, model, add_s, add_r, ps, pr, ds, dr, mod, buoy):
    below, above = inner_tile()
    mod[4:12] = model[0]
    buoy[4:12] = model[1]
    ps[0, 0:4] = below(prev[0:4])
    ps[0, 4:12] = own[0]
    ps[0, 12:16] = above(nxt[0:4])
    pr[0, 1:4] = below(prev[8:11])
    pr[0, 4:12] = own[2]
    pr[0, 12:15] = above(nxt[7:10])
    for d, f, at, vy, after in ((ds, 0, 4, 7, 4), (dr, 1, 11, 14, 10)):
        d[1:4] = below(prev[at : at + 3])
        d[4] = own[2 * f + 1, 0] - below(prev[vy])
        d[5:12] = own[2 * f + 1, 1:8]
        d[12] = above(nxt[after] - mine[vy])
        d[13:15] = above(nxt[after + 1 : after + 3])
    run, first = stepper(ps, pr, ds, dr, mod, buoy, add_s, add_r)
    first(4, 12)
    run(0, [(5, (0,)), (8, (0,))], 3)
    run(0, [(11, (0,))], 1, 1)
    run(1, [(6, (0, 1)), (8, (0, 1))], 2)
    run(1, [(5, (1,)), (10, (0, 1))], 1, 1)
    run(2, [(7, (0, 1)), (8, (0, 1))], 1, 1)
    run(2, [(6, (1,)), (9, (0, 1))], 1, 1)
    run(3, [(7, (1,)), (8, (0, 1))], 1, 1)


def outer_kernel(
    anchors, model_prev, model_next, add_s, add_r, ps_in, pr_in, ds_in, dr_in, mod_in, buoy_in,
    keep, send, send_far, ps, pr, ds, dr, mod, buoy, corr,
):
    del ps_in, pr_in, ds_in, dr_in, mod_in, buoy_in
    below, above = inner_tile()
    mod[1:4] = below(model_prev[0:3])
    mod[12:15] = above(model_next[0:3])
    buoy[0:4] = below(model_prev[3:7])
    buoy[12:15] = above(model_next[3:6])
    keep[...] = jnp.zeros(keep.shape, F32)
    send[...] = jnp.zeros(send.shape, F32)
    send_far[...] = jnp.zeros(send_far.shape, F32)
    run, first = stepper(ps, pr, ds, dr, mod, buoy, add_s, add_r)
    first(1, 4)
    first(12, 15)
    for s in range(STEPS):
        both = (0, 1) if s else (0,)
        run(s, [(s + 1, both), (12 - s, both), (s + 4, (0,))], 1, 1)
        run(s, [(s + 2, both), (13 - s, both)], 2, INLINE)

    def image(y, _):
        value = ps[4, y] * (pr[1, y] + add_r[3, y]) + ps[3, y] * (pr[2, y] + add_r[2, y])
        value += ps[2, y] * (pr[3, y] + add_r[1, y]) + ps[1, y] * (pr[4, y] + add_r[0, y])
        corr[pl.ds(y - STEPS, ROWS, stride=COLS), :] = value / STEPS
        return 0

    lax.fori_loop(STEPS, STEPS + COLS, image, 0, unroll=8)

    c, g = place()
    b = anchor(anchors, g)
    odd = (c + b) & 1
    x = lax.axis_index("x")
    for i in range(8):
        keep[((b + odd) >> 1) + i] = corr[pl.ds(pl.multiple_of(32 * (odd + 2 * i), 32), 32), :]
        k = 1 - odd + 2 * i
        j = (b + k) >> 1
        d = ((j >> 2) - x) & (NX - 1)

        @pl.when(d == 2)
        def _(k=k, j=j):
            send_far[j & (NZH - 1)] = corr[pl.ds(pl.multiple_of(32 * k, 32), 32), :]

        @pl.when(d != 2)
        def _(k=k, j=j, d=d):
            send[jnp.minimum(d, 2) * NZH + (j & (NZH - 1))] = corr[pl.ds(pl.multiple_of(32 * k, 32), 32), :]


STATE = [shape(STEPS + 1, PLANES, ROWS, DEPTH)] * 2 + [shape(PLANES, ROWS, DEPTH)] * 4


def inner(*operands):
    return pl.pallas_call(
        inner_kernel,
        out_shape=STATE,
        in_specs=[VMEM] * 7,
        out_specs=[VMEM] * 6,
        compiler_params=params(4),
        cost_estimate=COST,
        name="inner",
    )(*operands)


def outer(*operands):
    return pl.pallas_call(
        outer_kernel,
        out_shape=[shape(16, 32, DEPTH), shape(12, 32, DEPTH), shape(4, 32, DEPTH)] + STATE,
        in_specs=[VMEM] * 11,
        out_specs=[VMEM] * 9,
        scratch_shapes=[pltpu.VMEM((COLS * ROWS, DEPTH), F32)],
        input_output_aliases={5 + i: 3 + i for i in range(6)},
        compiler_params=params(4),
        name="outer",
    )(*operands)[:3]


def halve_kernel(distances, keep, got, *outs):
    x = lax.axis_index("x")
    for at, (d, out) in enumerate(zip(distances, outs)):
        for i in range(NZH):
            out[i] = keep[((x + d) & (NX - 1)) * NZH + i] + got[at * NZH + i]


def quarter_kernel(s0, r1, r2, r3, u0, u1, u2, u3):
    z = lax.axis_index("zh")
    for d, out in enumerate((u0, u1, u2, u3)):
        at = (z + d) & (NZH - 1)
        out[...] = (s0[at] + r1[at]) + (r2[at] + r3[at])


def last_kernel(u0, q1, q2, q3, out):
    out[...] = (u0[...] + q1[...]) + (q2[...] + q3[...])


def other_core(block):
    return lax.ppermute(block, "core", [(0, 1), (1, 0)])


def to_tile(block, distance):
    return lax.ppermute(block, "tile", [(i, (i + distance) % NT) for i in range(NT)])


def along(blocks, axis, order):
    return [lax.ppermute(blocks[d - 1], axis, [(i, (i + d) % 4) for i in range(4)]) for d in order]


def local(velocity, density, anchors, src_state, rcv_state, src_pos, wavelet, rec_pos, traces):
    plane = (ROWS, DEPTH)
    strip = jnp.stack([velocity, density])[None]
    zs = along([strip] * 3, "zh", GATHER)

    own, to_prev, to_next, anchors = pl.pallas_call(
        pack_kernel,
        out_shape=[
            shape(4, COLS * ROWS, DEPTH),
            shape(13, *plane),
            shape(15, *plane),
            jax.ShapeDtypeStruct((1, *anchors.shape), anchors.dtype),
        ],
        in_specs=[HBM] * 3,
        out_specs=[VMEM] * 4,
        scratch_shapes=[
            pltpu.VMEM((4, ROWS, COLS, DEPTH), F32),
            pltpu.VMEM((4, ROWS, COLS, DEPTH), F32),
            pltpu.SemaphoreType.DMA((2, 2)),
            pltpu.SemaphoreType.DMA,
        ],
        compiler_params=params(8),
        name="pack",
    )(*(pltpu.with_memory_space_constraint(a, pltpu.HBM) for a in (src_state, rcv_state, anchors[None])))
    *zs, own, to_prev, to_next = lax.optimization_barrier((*zs, own, to_prev, to_next))

    xs = [jnp.concatenate([strip, *zs])]
    xs += along([xs[0]] * 3, "x", GATHER)

    halo_next = to_tile(to_prev, -1)
    halo_prev = to_tile(to_next, 1)

    inj_src, inj_rec = pl.pallas_call(
        inject_kernel,
        out_shape=[shape(STEPS, PLANES, *plane)] * 2,
        in_specs=[SMEM] * 4,
        out_specs=[VMEM] * 2,
        compiler_params=params(2),
        name="inject",
    )(src_pos, wavelet[0].T, rec_pos, traces[0].T)

    other, mine = [
        pl.pallas_call(
            functools.partial(window_kernel, offset),
            out_shape=[shape(8, *strip.shape[2:])] * 2,
            in_specs=[VMEM] * 5,
            out_specs=[VMEM] * 2,
            compiler_params=params(2),
            name="window%d" % offset,
        )(anchors, *xs)
        for offset in (1, 0)
    ]
    model = (anchors, *mine, *(other_core(block) for block in other))
    edge_prev, edge_next = pl.pallas_call(
        edge_kernel,
        out_shape=[shape(6 * ROWS, DEPTH), shape(7 * ROWS, DEPTH)],
        in_specs=[VMEM] * 5,
        out_specs=[VMEM] * 2,
        compiler_params=params(2),
        name="edge",
    )(*model)
    model_next = to_tile(edge_prev.reshape(6, *plane), -1)
    model_prev = to_tile(edge_next.reshape(7, *plane), 1)
    mb = pl.pallas_call(
        model_kernel,
        out_shape=shape(2, COLS * ROWS, DEPTH),
        in_specs=[VMEM] * 5,
        out_specs=VMEM,
        compiler_params=params(2),
        name="model",
    )(*model)

    state = inner(
        own.reshape(4, COLS, *plane),
        halo_prev,
        halo_next,
        to_next,
        mb.reshape(2, COLS, *plane),
        inj_src,
        inj_rec,
    )
    keep, send, send_far = outer(anchors, model_prev, model_next, inj_src, inj_rec, *state)

    def halve(distances, block):
        return pl.pallas_call(
            functools.partial(halve_kernel, distances),
            out_shape=[shape(NZH, 32, DEPTH)] * len(distances),
            in_specs=[VMEM, VMEM],
            out_specs=[VMEM] * len(distances),
            compiler_params=params(2),
            name="halve%d" % len(distances),
        )(keep, other_core(block))

    (far,) = halve((2,), send_far)
    stay, after, before = halve((0, 1, 3), send)
    parts = [stay, after, far, before]
    moved = along(parts[1:], "x", SCATTER)
    parts = pl.pallas_call(
        quarter_kernel,
        out_shape=[shape(32, DEPTH)] * NZH,
        in_specs=[VMEM] * NX,
        out_specs=[VMEM] * NZH,
        compiler_params=params(2),
        name="quarter",
    )(parts[0], *moved)
    moved = along(parts[1:], "zh", SCATTER)
    image = pl.pallas_call(
        last_kernel,
        out_shape=shape(32, DEPTH),
        in_specs=[VMEM] * NZH,
        out_specs=VMEM,
        compiler_params=params(2),
        name="last",
    )(parts[0], *moved)
    return image.reshape(velocity.shape)


def solution(mesh):
    shot = ("x", "zh", "core")
    return jax.shard_map(
        local,
        mesh=Mesh(mesh.devices.reshape(NX, NZH, NC, NT), (*shot, "tile")),
        in_specs=(
            P(shot, "tile", None),
            P(shot, "tile", None),
            P(),
            P(None, shot, "tile", None),
            P(None, shot, "tile", None),
            P(shot, None),
            P(shot, None, None),
            P(shot, None),
            P(shot, None, None),
        ),
        out_specs=P(shot, "tile", None),
        check_vma=False,
    )
```

```python
import functools

import jax
import jax.numpy as jnp
from jax import lax
from jax.experimental import pallas as pl
from jax.experimental.pallas import tpu as pltpu
from jax.sharding import Mesh
from jax.sharding import PartitionSpec as P

STEPS = 4
INLINE = 1
COST = None
GATHER, SCATTER = (3, 1, 2), (2, 1, 3)
F32 = jnp.float32
ROWS = 64
COLS = 8
DEPTH = 128
PLANES = COLS + 2 * STEPS
NX, NZH, NC, NT = 4, 4, 2, 8

VMEM = pl.BlockSpec(memory_space=pltpu.VMEM)
SMEM = pl.BlockSpec(memory_space=pltpu.SMEM)
ANY = pl.BlockSpec(memory_space=pl.ANY)
HBM = pl.BlockSpec(memory_space=pltpu.HBM)


def shape(*dims):
    return jax.ShapeDtypeStruct(dims, F32)


def params(mib):
    return pltpu.CompilerParams(vmem_limit_bytes=mib * 1024 * 1024)


def place():
    c = lax.axis_index("core")
    return c, (lax.axis_index("x") * NZH + lax.axis_index("zh")) * NC + c


def anchor(anchors, g):
    lane = lax.broadcasted_iota(jnp.int32, anchors.shape, 1)
    return jnp.sum(jnp.where(lane == g, anchors[...], 0))


def first_strip(b, c):
    return (b + ((c + b) & 1)) >> 1


def pack_kernel(src_in, rcv_in, anchors_in, own, to_prev, to_next, anchors, src, rcv, sem, anchors_sem):
    held = pltpu.make_async_copy(anchors_in, anchors, anchors_sem)
    held.start()
    half = ROWS // 2
    copies = []
    for h in range(2):
        cut = slice(h * half, h * half + half)
        for f, (a, b) in enumerate(((src_in, src), (rcv_in, rcv))):
            copies.append(pltpu.make_async_copy(a.at[:, cut], b.at[:, cut], sem.at[h, f]))
            copies[-1].start()
    lane = lax.broadcasted_iota(jnp.int32, (COLS, DEPTH), 1)
    col = lax.broadcasted_iota(jnp.int32, (COLS, DEPTH), 0)

    def row(x, before):
        after = []
        for f, state in enumerate((src, rcv)):
            p, vx, vy, vz = (state[i, x] for i in range(4))
            spread = vx - before[f]
            spread += vy - jnp.where(col == 0, 0.0, pltpu.roll(vy, 1, 0))
            spread += vz - jnp.where(lane == 0, 0.0, pltpu.roll(vz, 1, 1))
            own[2 * f, pl.ds(x, COLS, stride=ROWS), :] = p
            own[2 * f + 1, pl.ds(x, COLS, stride=ROWS), :] = spread
            to_next[7 + 7 * f, pl.ds(x, 1), :] = vy[COLS - 1 :, :]
            after.append(vx)
        return tuple(after)

    before = (jnp.zeros((COLS, DEPTH), F32),) * 2
    for h in range(2):
        for copy in copies[2 * h : 2 * h + 2]:
            copy.wait()
        before = lax.fori_loop(h * half, h * half + half, row, before, unroll=8)

    held.wait()

    def plane(f, y):
        return own[f, y * ROWS : (y + 1) * ROWS, :]

    for i, (f, y) in enumerate(
        [(0, 0), (0, 1), (0, 2), (0, 3), (1, 0), (1, 1), (1, 2)]
        + [(2, 0), (2, 1), (2, 2), (3, 0), (3, 1), (3, 2)]
    ):
        to_prev[i] = plane(f, y)
    for i, (f, y) in (
        list(enumerate([(0, 4), (0, 5), (0, 6), (0, 7), (1, 5), (1, 6), (1, 7)]))
        + list(enumerate([(2, 5), (2, 6), (2, 7), (3, 5), (3, 6), (3, 7)], 8))
    ):
        to_next[i] = plane(f, y)


def inject_kernel(src_pos, wavelet, rec_pos, traces, src_out, rec_out):
    for out in (src_out, rec_out):
        for s in range(STEPS):
            out[s, 1 : PLANES - 1] = jnp.zeros((PLANES - 2, ROWS, DEPTH), F32)
    first = lax.axis_index("tile") * COLS - STEPS
    lane = lax.broadcasted_iota(jnp.int32, (1, DEPTH), 1)
    for pos, amp, out in ((src_pos, wavelet, src_out), (rec_pos, traces, rec_out)):

        def point(k, _, pos=pos, amp=amp, out=out):
            cell = pos[0, k]
            x = cell >> 13
            y = jnp.clip(((cell >> 7) & (COLS * NT - 1)) - first, 0, PLANES - 1)
            hit = lane == (cell & (DEPTH - 1))
            old = [out[s, y, pl.ds(x, 1), :] for s in range(STEPS)]
            for s in range(STEPS):
                out[s, y, pl.ds(x, 1), :] = old[s] + jnp.where(hit, amp[s, k], 0.0)
            return 0

        lax.fori_loop(0, pos.shape[1], point, 0, unroll=8)


def window_kernel(offset, anchors, a0, a1, a2, a3, modulus, buoyancy):
    x, z = lax.axis_index("x"), lax.axis_index("zh")
    c, g = place()
    first = first_strip(anchor(anchors, g + offset * (1 - 2 * c)), c)
    for dx, strips in zip((0, *GATHER), (a0, a1, a2, a3)):
        for dz, at in zip((0, *GATHER), range(NZH)):
            i = ((x - dx) & (NX - 1)) * NZH + ((z - dz) & (NZH - 1)) - first

            @pl.when((i >= 0) & (i < 8))
            def _(i=i, strips=strips, at=at):
                vel, den = strips[at, 0], strips[at, 1]
                modulus[i] = den * vel * vel
                buoyancy[i] = 1.0 / den


def strip_rows(anchors, own_m, own_b, other_m, other_b):
    c, g = place()
    odd = (c + anchor(anchors, g)) & 1
    for m, b, start in ((own_m, own_b, odd), (other_m, other_b, 1 - odd)):
        for i in range(8):
            for r in range(4):
                yield 4 * (start + 2 * i) + r, m[i, r], b[i, r]


def edge_kernel(anchors, own_m, own_b, other_m, other_b, to_prev, to_next):
    for x, m, b in strip_rows(anchors, own_m, own_b, other_m, other_b):
        to_prev[pl.ds(x, 3, stride=ROWS), :] = m[:3]
        to_prev[pl.ds(x + 3 * ROWS, 3, stride=ROWS), :] = b[:3]
        to_next[pl.ds(x, 3, stride=ROWS), :] = m[5:]
        to_next[pl.ds(x + 3 * ROWS, 4, stride=ROWS), :] = b[4:]


def model_kernel(anchors, own_m, own_b, other_m, other_b, out):
    for x, m, b in strip_rows(anchors, own_m, own_b, other_m, other_b):
        out[0, pl.ds(x, COLS, stride=ROWS), :] = m
        out[1, pl.ds(x, COLS, stride=ROWS), :] = b


def inner_tile():
    tile = lax.axis_index("tile")
    low, high = tile > 0, tile < NT - 1
    return (lambda value: jnp.where(low, value, 0.0)), (lambda value: jnp.where(high, value, 0.0))


def stepper(ps, pr, ds, dr, mod, buoy, add_s, add_r):
    lane = lax.broadcasted_iota(jnp.int32, (8, DEPTH), 1)
    row = lax.broadcasted_iota(jnp.int32, (8, DEPTH), 0)
    first_lane, last_lane, first_row, last_row = lane == 0, lane == DEPTH - 1, row == 0, row == 7
    blocks = range(ROWS // 8)
    zero = jnp.zeros((8, DEPTH), F32)
    fields = ((ps, ds, add_s, lambda s: s), (pr, dr, add_r, lambda s: STEPS - s))

    def get(ref, *at):
        return [ref[(*at, slice(8 * v, 8 * v + 8))] for v in blocks]

    def spread_of(p, after, before, b):
        down = [pltpu.roll(p[v], 7, 0) for v in blocks] + [zero]
        flux_y = [b[v] * (after[v] - p[v]) for v in blocks]
        out, last = [], zero
        for v in blocks:
            flux_x = b[v] * (jnp.where(last_row, down[v + 1], down[v]) - p[v])
            flux_z = b[v] * (jnp.where(last_lane, 0.0, pltpu.roll(p[v], DEPTH - 1, 1)) - p[v])
            turned = pltpu.roll(flux_x, 1, 0)
            spread = (flux_x - jnp.where(first_row, last, turned)) + (flux_y[v] - before[v])
            spread += flux_z - jnp.where(first_lane, 0.0, pltpu.roll(flux_z, 1, 1))
            last = turned
            out.append(spread)
        return out, flux_y

    def plane(s, y, wanted, carry):
        m, b = get(mod, y), get(buoy, y)
        ends = []
        for f, (p, before) in zip(wanted, carry):
            p_all, d_all, add, amp = fields[f]
            after = get(p_all, s, y + 1)
            spread, flux = spread_of(p, after, before, b)
            ends.append((after, flux))
            for v in blocks:
                cut = slice(8 * v, 8 * v + 8)
                d = d_all[y, cut] - spread[v]
                p_all[s + 1, y, cut] = p[v] + add[amp(s), y, cut] - m[v] * d
                if s < STEPS - 1:
                    d_all[y, cut] = d
        return ends

    def run(s, groups, count, inline=0):
        carry = []
        for y, wanted in groups:
            b, part = get(buoy, y - 1), []
            for f in wanted:
                here, before = get(fields[f][0], s, y), get(fields[f][0], s, y - 1)
                part.append((here, [b[v] * (here[v] - before[v]) for v in blocks]))
            carry.append(part)

        def planes(i, carry):
            return [plane(s, y + i, wanted, part) for (y, wanted), part in zip(groups, carry)]

        if inline:
            for i in range(count):
                carry = planes(i, carry)
        else:
            lax.fori_loop(0, count, planes, carry)

    def first(low, high):
        for y in range(low, high):
            for v in blocks:
                cut = slice(8 * v, 8 * v + 8)
                pr[1, y, cut] = pr[0, y, cut] - mod[y, cut] * dr[y, cut]

    return run, first


def inner_kernel(own, prev, nxt, mine, model, add_s, add_r, ps, pr, ds, dr, mod, buoy):
    below, above = inner_tile()
    mod[4:12] = model[0]
    buoy[4:12] = model[1]
    ps[0, 0:4] = below(prev[0:4])
    ps[0, 4:12] = own[0]
    ps[0, 12:16] = above(nxt[0:4])
    pr[0, 1:4] = below(prev[8:11])
    pr[0, 4:12] = own[2]
    pr[0, 12:15] = above(nxt[7:10])
    for d, f, at, vy, after in ((ds, 0, 4, 7, 4), (dr, 1, 11, 14, 10)):
        d[1:4] = below(prev[at : at + 3])
        d[4] = own[2 * f + 1, 0] - below(prev[vy])
        d[5:12] = own[2 * f + 1, 1:8]
        d[12] = above(nxt[after] - mine[vy])
        d[13:15] = above(nxt[after + 1 : after + 3])
    run, first = stepper(ps, pr, ds, dr, mod, buoy, add_s, add_r)
    first(4, 12)
    run(0, [(5, (0,)), (8, (0,))], 3)
    run(0, [(11, (0,))], 1, 1)
    run(1, [(6, (0, 1)), (8, (0, 1))], 2)
    run(1, [(5, (1,)), (10, (0, 1))], 1, 1)
    run(2, [(7, (0, 1)), (8, (0, 1))], 1, 1)
    run(2, [(6, (1,)), (9, (0, 1))], 1, 1)
    run(3, [(7, (1,)), (8, (0, 1))], 1, 1)


def outer_kernel(
    anchors, model_prev, model_next, add_s, add_r, ps_in, pr_in, ds_in, dr_in, mod_in, buoy_in,
    keep, send, ps, pr, ds, dr, mod, buoy, corr,
):
    del ps_in, pr_in, ds_in, dr_in, mod_in, buoy_in
    below, above = inner_tile()
    mod[1:4] = below(model_prev[0:3])
    mod[12:15] = above(model_next[0:3])
    buoy[0:4] = below(model_prev[3:7])
    buoy[12:15] = above(model_next[3:6])
    keep[...] = jnp.zeros(keep.shape, F32)
    send[...] = jnp.zeros(send.shape, F32)
    run, first = stepper(ps, pr, ds, dr, mod, buoy, add_s, add_r)
    first(1, 4)
    first(12, 15)
    for s in range(STEPS):
        both = (0, 1) if s else (0,)
        run(s, [(s + 1, both), (12 - s, both), (s + 4, (0,))], 1, 1)
        run(s, [(s + 2, both), (13 - s, both)], 2, INLINE)

    def image(y, _):
        value = ps[4, y] * (pr[1, y] + add_r[3, y]) + ps[3, y] * (pr[2, y] + add_r[2, y])
        value += ps[2, y] * (pr[3, y] + add_r[1, y]) + ps[1, y] * (pr[4, y] + add_r[0, y])
        corr[pl.ds(y - STEPS, ROWS, stride=COLS), :] = value / STEPS
        return 0

    lax.fori_loop(STEPS, STEPS + COLS, image, 0, unroll=8)

    c, g = place()
    b = anchor(anchors, g)
    odd = (c + b) & 1
    for out, start in ((keep, odd), (send, 1 - odd)):
        at = (b + start) >> 1
        for i in range(8):
            out[at + i] = corr[pl.ds(pl.multiple_of(32 * (start + 2 * i), 32), 32), :]


STATE = [shape(STEPS + 1, PLANES, ROWS, DEPTH)] * 2 + [shape(PLANES, ROWS, DEPTH)] * 4


def inner(*operands):
    return pl.pallas_call(
        inner_kernel,
        out_shape=STATE,
        in_specs=[VMEM] * 7,
        out_specs=[VMEM] * 6,
        compiler_params=params(4),
        cost_estimate=COST,
        name="inner",
    )(*operands)


def outer(*operands):
    return pl.pallas_call(
        outer_kernel,
        out_shape=[shape(16, 32, DEPTH)] * 2 + STATE,
        in_specs=[VMEM] * 11,
        out_specs=[VMEM] * 8,
        scratch_shapes=[pltpu.VMEM((COLS * ROWS, DEPTH), F32)],
        input_output_aliases={5 + i: 2 + i for i in range(6)},
        compiler_params=params(4),
        name="outer",
    )(*operands)[:2]


def halve_kernel(keep, got, s0, s1, s2, s3):
    x = lax.axis_index("x")
    for d, out in enumerate((s0, s1, s2, s3)):
        at = ((x + d) & (NX - 1)) * NZH
        for i in range(NZH):
            out[i] = keep[at + i] + got[at + i]


def quarter_kernel(s0, r1, r2, r3, u0, u1, u2, u3):
    z = lax.axis_index("zh")
    for d, out in enumerate((u0, u1, u2, u3)):
        at = (z + d) & (NZH - 1)
        out[...] = (s0[at] + r1[at]) + (r2[at] + r3[at])


def last_kernel(u0, q1, q2, q3, out):
    out[...] = (u0[...] + q1[...]) + (q2[...] + q3[...])


def other_core(block):
    return lax.ppermute(block, "core", [(0, 1), (1, 0)])


def to_tile(block, distance):
    return lax.ppermute(block, "tile", [(i, (i + distance) % NT) for i in range(NT)])


def along(blocks, axis, order):
    return [lax.ppermute(blocks[d - 1], axis, [(i, (i + d) % 4) for i in range(4)]) for d in order]


def local(velocity, density, anchors, src_state, rcv_state, src_pos, wavelet, rec_pos, traces):
    plane = (ROWS, DEPTH)
    strip = jnp.stack([velocity, density])[None]
    zs = along([strip] * 3, "zh", GATHER)

    own, to_prev, to_next, anchors = pl.pallas_call(
        pack_kernel,
        out_shape=[
            shape(4, COLS * ROWS, DEPTH),
            shape(13, *plane),
            shape(15, *plane),
            jax.ShapeDtypeStruct((1, *anchors.shape), anchors.dtype),
        ],
        in_specs=[HBM] * 3,
        out_specs=[VMEM] * 4,
        scratch_shapes=[
            pltpu.VMEM((4, ROWS, COLS, DEPTH), F32),
            pltpu.VMEM((4, ROWS, COLS, DEPTH), F32),
            pltpu.SemaphoreType.DMA((2, 2)),
            pltpu.SemaphoreType.DMA,
        ],
        compiler_params=params(8),
        name="pack",
    )(*(pltpu.with_memory_space_constraint(a, pltpu.HBM) for a in (src_state, rcv_state, anchors[None])))
    *zs, own, to_prev, to_next = lax.optimization_barrier((*zs, own, to_prev, to_next))

    xs = [jnp.concatenate([strip, *zs])]
    xs += along([xs[0]] * 3, "x", GATHER)

    halo_next = to_tile(to_prev, -1)
    halo_prev = to_tile(to_next, 1)

    inj_src, inj_rec = pl.pallas_call(
        inject_kernel,
        out_shape=[shape(STEPS, PLANES, *plane)] * 2,
        in_specs=[SMEM] * 4,
        out_specs=[VMEM] * 2,
        compiler_params=params(2),
        name="inject",
    )(src_pos, wavelet[0].T, rec_pos, traces[0].T)

    other, mine = [
        pl.pallas_call(
            functools.partial(window_kernel, offset),
            out_shape=[shape(8, *strip.shape[2:])] * 2,
            in_specs=[VMEM] * 5,
            out_specs=[VMEM] * 2,
            compiler_params=params(2),
            name="window%d" % offset,
        )(anchors, *xs)
        for offset in (1, 0)
    ]
    model = (anchors, *mine, *(other_core(block) for block in other))
    edge_prev, edge_next = pl.pallas_call(
        edge_kernel,
        out_shape=[shape(6 * ROWS, DEPTH), shape(7 * ROWS, DEPTH)],
        in_specs=[VMEM] * 5,
        out_specs=[VMEM] * 2,
        compiler_params=params(2),
        name="edge",
    )(*model)
    model_next = to_tile(edge_prev.reshape(6, *plane), -1)
    model_prev = to_tile(edge_next.reshape(7, *plane), 1)
    mb = pl.pallas_call(
        model_kernel,
        out_shape=shape(2, COLS * ROWS, DEPTH),
        in_specs=[VMEM] * 5,
        out_specs=VMEM,
        compiler_params=params(2),
        name="model",
    )(*model)

    state = inner(
        own.reshape(4, COLS, *plane),
        halo_prev,
        halo_next,
        to_next,
        mb.reshape(2, COLS, *plane),
        inj_src,
        inj_rec,
    )
    keep, send = outer(anchors, model_prev, model_next, inj_src, inj_rec, *state)

    parts = pl.pallas_call(
        halve_kernel,
        out_shape=[shape(NZH, 32, DEPTH)] * NX,
        in_specs=[VMEM, VMEM],
        out_specs=[VMEM] * NX,
        compiler_params=params(2),
        name="halve",
    )(keep, other_core(send))
    moved = along(parts[1:], "x", SCATTER)
    parts = pl.pallas_call(
        quarter_kernel,
        out_shape=[shape(32, DEPTH)] * NZH,
        in_specs=[VMEM] * NX,
        out_specs=[VMEM] * NZH,
        compiler_params=params(2),
        name="quarter",
    )(parts[0], *moved)
    moved = along(parts[1:], "zh", SCATTER)
    image = pl.pallas_call(
        last_kernel,
        out_shape=shape(32, DEPTH),
        in_specs=[VMEM] * NZH,
        out_specs=VMEM,
        compiler_params=params(2),
        name="last",
    )(parts[0], *moved)
    return image.reshape(velocity.shape)


def solution(mesh):
    shot = ("x", "zh", "core")
    return jax.shard_map(
        local,
        mesh=Mesh(mesh.devices.reshape(NX, NZH, NC, NT), (*shot, "tile")),
        in_specs=(
            P(shot, "tile", None),
            P(shot, "tile", None),
            P(),
            P(None, shot, "tile", None),
            P(None, shot, "tile", None),
            P(shot, None),
            P(shot, None, None),
            P(shot, None),
            P(shot, None, None),
        ),
        out_specs=P(shot, "tile", None),
        check_vma=False,
    )
```
